256 devices in a mesh: leaf: 256 (over y, z, x, core).
Axes of the slice: x: 4, y: 4, z: 8, core: 2. Of those that a mesh axis runs over, the one named last changes fastest.
Arguments:
- measured: bfloat16 [16, 1048576], P(None, 'leaf'), may hold values from -6 to 6
- cluster_perm: int32 [256, 4096], P('leaf'), may hold values from 0 to 4095, each once within a row
- near_offsets: int32 [16384, 4], P('leaf'), may hold values from -2 to 2
- near_blocks: bfloat16 [16384, 64, 256], P('leaf'), may hold values from -0.375 to 0.375
- leaf_bases: bfloat16 [16384, 4096], P('leaf'), may hold values from -0.75 to 0.75
- local_transfer: bfloat16 [16128, 64, 128], P('leaf'), may hold values from -0.5 to 0.5
- coupling_pattern: int32 [32256, 2], P('leaf'), may hold values from 2 to 127, as said below
- local_coupling: bfloat16 [32256, 64, 128], P('leaf'), as said below
- root_transfer: bfloat16 [256, 4096], P('leaf'), may hold values from -0.5 to 0.5
- top_blocks: bfloat16 [256, 64, 128], replicated, as said below
Outputs:
- covariance_product: float32 [16, 1048576], P(None, 'leaf')
The draws below stay inside these ranges and needn't reach their ends.
Inputs may be any that keep to these rules, and one draw needn't show every extreme that they name: `coupling_pattern`: row d * 126 + s - 2 belongs to slot s of subtree d; its entries are other slots of the same depth in that subtree. `local_coupling`: coupling blocks of the slots of each subtree in heap order. `top_blocks`: row 0 and the transfer half of row 1 are not used.
All inputs are finite; a program needn't handle non-finite values.
Results may differ from the reference program's by a relative error of at most 0.00065.
Values may be sent and summed in bfloat16 or wider, within the bound.
A program may use at most 128 MiB of HBM per device.

```python
import math
import jax
import jax.numpy as jnp
from jax import lax

LEAF = 64
RANK = 64
NRHS = 16
NEAR = 4
RANGE = 2
COUP = 2
LEAVES_DEV = 64
LOCAL_LEVELS = 6
TOP_LEVELS = 8
LNODES = 126
PTS_DEV = 4096
POINTS = 1048576
N_LEAF = 256


def slot_depth(node_slots):
    thresholds = jnp.left_shift(jnp.int32(1), jnp.arange(1, 24, dtype=jnp.int32))
    return jnp.sum((node_slots[:, None] >= thresholds[None, :]).astype(jnp.int32), axis=1)


def draw_coupling_pattern(key, part):
    key = jax.random.fold_in(key, 11)
    node_slots = jnp.arange(N_LEAF * LNODES, dtype=jnp.int32) % LNODES + 2
    level_span = jnp.left_shift(jnp.int32(1), slot_depth(node_slots))
    position = node_slots - level_span
    random_ints = jax.random.randint(key, (N_LEAF * LNODES, COUP), 0, 1 << 20, dtype=jnp.int32)
    offset_now = random_ints % jnp.maximum(level_span - 1, 1)[:, None] + 1
    partner = level_span[:, None] + (position[:, None] + offset_now) % level_span[:, None]
    column = jnp.arange(COUP, dtype=jnp.int32)[None, :]
    partner = jnp.where((position[:, None] == 0) & (column == 0), 2 * level_span[:, None] - 1, partner)
    return partner.astype(jnp.int32)


def draw_local_coupling(key, part):
    key = jax.random.fold_in(key, 12)
    node_slots = jnp.arange(N_LEAF * LNODES, dtype=jnp.int32) % LNODES + 2
    levels_down = (LOCAL_LEVELS - slot_depth(node_slots)).astype(jnp.float32)
    factor = jnp.exp2(0.5 * levels_down) / math.sqrt(COUP * RANK)
    values = jax.random.truncated_normal(key, -4.0, 4.0, (N_LEAF * LNODES, RANK, COUP * RANK), jnp.float32)
    return (values * factor[:, None, None]).astype(jnp.bfloat16)


def draw_top_blocks(key, part):
    key = jax.random.fold_in(key, 13)
    heap_nodes = jnp.arange(N_LEAF, dtype=jnp.int32)
    levels_down = (LOCAL_LEVELS + TOP_LEVELS - 1 - slot_depth(heap_nodes)).astype(jnp.float32)
    coupling_scale = jnp.exp2(0.5 * levels_down) / math.sqrt(RANK)
    column = jnp.arange(2 * RANK, dtype=jnp.int32)
    scales = jnp.where(column[None, :] < RANK, coupling_scale[:, None], 1.0 / math.sqrt(2 * RANK))
    values = jax.random.truncated_normal(key, -4.0, 4.0, (N_LEAF, RANK, 2 * RANK), jnp.float32)
    return (values * scales[:, None, :]).astype(jnp.bfloat16)


def plant(entries, rng, low, top_value):
    dims = entries.shape
    index_at = [jax.random.randint(jax.random.fold_in(rng, axis), (), 0, dims[axis]) for axis in range(len(dims))]
    entries = entries.at[tuple(index_at)].set(low)
    longest = dims.index(max(dims))
    index_at[longest] = (index_at[longest] + 1) % dims[longest]
    return entries.at[tuple(index_at)].set(top_value)


def steps_of(rng, shape, cuts, low, largest):
    def one(axis_at, shards_of):
        draws = jax.random.uniform(jax.random.fold_in(jax.random.fold_in(rng, 6), axis_at), (shards_of,), jnp.float32, low / len(cuts), largest / len(cuts))
        return jnp.repeat(jnp.exp(draws), shape[axis_at] // shards_of).reshape((-1,) + (1,) * (len(shape) - axis_at - 1))

    gain = one(*cuts[0])
    for cut in cuts[1:]:
        gain = gain * one(*cut)
    return gain


def centred(own_key, shape, width, reach, pieces=(), kind=jnp.bfloat16):
    array = jax.random.normal(own_key, shape, jnp.float32) * width
    if len(pieces) > 0:
        array = steps_of(own_key, shape, pieces, -0.22, 0.18) * array
    return jnp.clip(array, min=-reach, max=reach).astype(kind)


def setup_inputs(seed: int = 0) -> dict:
    splits = jax.random.split(jax.random.key(seed), 11)
    measured = centred(splits[0], (NRHS, POINTS), 1.0, 6.0, ((1, 256),))
    cluster_perm = jax.vmap(lambda own: jax.random.permutation(own, PTS_DEV))(jax.random.split(splits[1], N_LEAF)).reshape((N_LEAF, PTS_DEV)).astype(jnp.int32)
    near_offsets = plant(jax.random.randint(splits[2], (N_LEAF * LEAVES_DEV, NEAR), -RANGE, RANGE + 1), jax.random.fold_in(splits[2], 1), -RANGE, RANGE).astype(jnp.int32)
    near_blocks = centred(splits[3], (N_LEAF * LEAVES_DEV, LEAF, NEAR * LEAF), (NEAR * LEAF) ** -0.5, 0.375, ((0, 256),))
    leaf_bases = centred(splits[4], (N_LEAF * LEAVES_DEV, LEAF * RANK), LEAF ** -0.5, 0.75, ((0, 256),))
    local_transfer = centred(splits[5], (N_LEAF * (LEAVES_DEV - 1), RANK, 2 * RANK), (2 * RANK) ** -0.5, 0.5, ((0, 256),))
    coupling_pattern = draw_coupling_pattern(jax.random.fold_in(splits[10], 71), 0)
    local_coupling = draw_local_coupling(jax.random.fold_in(splits[10], 71), 0)
    root_transfer = centred(splits[8], (N_LEAF, RANK * RANK), (2 * RANK) ** -0.5, 0.5, ((0, 256),))
    top_blocks = draw_top_blocks(jax.random.fold_in(splits[10], 71), 0)
    return dict(measured=measured, cluster_perm=cluster_perm, near_offsets=near_offsets, near_blocks=near_blocks, leaf_bases=leaf_bases, local_transfer=local_transfer, coupling_pattern=coupling_pattern, local_coupling=local_coupling, root_transfer=root_transfer, top_blocks=top_blocks)


def climb_level(coeffs, pairing, groups):
    merged = coeffs.reshape(coeffs.shape[0], groups, 2, coeffs.shape[-1])
    return jnp.einsum("rpci,picj->rpj", merged, pairing, precision=lax.Precision.HIGHEST)


def subtree_up(points, basis_rows, pairings):
    leaf_basis = basis_rows.reshape(LEAVES_DEV, LEAF, RANK).astype(jnp.float32)
    current = jnp.einsum("rlp,lpk->rlk", points.reshape(NRHS, LEAVES_DEV, LEAF).astype(jnp.float32), leaf_basis, precision=lax.Precision.HIGHEST)
    by_level = [current]
    for level_now in range(LOCAL_LEVELS - 1, -1, -1):
        groups = 2 ** level_now
        current = climb_level(current, pairings[groups - 1:2 * groups - 1], groups)
        by_level.insert(0, current)
    return by_level


def reference(measured, cluster_perm, near_offsets, near_blocks, leaf_bases, local_transfer, coupling_pattern, local_coupling, root_transfer, top_blocks):
    highest = lax.Precision.HIGHEST
    devices = N_LEAF
    per_device = measured.reshape(NRHS, devices, PTS_DEV).transpose(1, 0, 2)
    clustered = jax.vmap(lambda rows_here, order_here: rows_here[:, order_here])(per_device, cluster_perm)
    basis_all = leaf_bases.reshape(devices, LEAVES_DEV, LEAF * RANK)
    pairing_all = local_transfer.reshape(devices, LEAVES_DEV - 1, RANK, 2 * RANK)

    def root_of(items):
        points, basis_rows, pair_rows = items
        pairings = pair_rows.astype(jnp.float32).reshape(LEAVES_DEV - 1, RANK, 2, RANK)
        return subtree_up(points, basis_rows, pairings)[0][:, 0, :]

    roots_all = lax.map(root_of, (clustered, basis_all, pairing_all))
    root_maps = root_transfer.reshape(devices, RANK, RANK).astype(jnp.float32)
    top_table = top_blocks.astype(jnp.float32)
    levels_top = {TOP_LEVELS: roots_all}
    climbing = jnp.einsum("nij,nri->nrj", root_maps, roots_all, precision=highest)
    for level_now in range(TOP_LEVELS - 1, 0, -1):
        groups = 2 ** level_now
        parents = climbing[0::2] + climbing[1::2]
        levels_top[level_now] = parents
        climbing = jnp.einsum("nij,nri->nrj", top_table[groups:2 * groups, :, RANK:], parents, precision=highest)
    field_now = jnp.zeros((1, NRHS, RANK), jnp.float32)
    for level_now in range(1, TOP_LEVELS + 1):
        groups = 2 ** (level_now - 1)
        pair_blocks = top_table[groups:2 * groups, :, :RANK]
        left_side = levels_top[level_now][0::2]
        right_side = levels_top[level_now][1::2]
        to_left = jnp.einsum("hij,hrj->hri", pair_blocks, right_side, precision=highest)
        to_right = jnp.einsum("hji,hrj->hri", pair_blocks, left_side, precision=highest)
        coupled = jnp.stack([to_left, to_right], 1).reshape(2 * groups, NRHS, RANK)
        if level_now == TOP_LEVELS:
            maps_now = root_maps
        else:
            maps_now = top_table[2 * groups:4 * groups, :, RANK:]
        from_above = jnp.einsum("nij,nrj->nri", maps_now, jnp.repeat(field_now, 2, axis=0), precision=highest)
        field_now = coupled + from_above
    fields_root = field_now

    padded = jnp.pad(clustered.transpose(1, 0, 2).reshape(NRHS, devices * LEAVES_DEV, LEAF), ((0, 0), (RANGE, RANGE), (0, 0)))

    def finish(items):
        index_now, points, basis_rows, pair_rows, offsets, blocks, pattern, coupling_rows, field_root, order_here = items
        pairings = pair_rows.astype(jnp.float32).reshape(LEAVES_DEV - 1, RANK, 2, RANK)
        by_level = subtree_up(points, basis_rows, pairings)
        stacked = jnp.concatenate(by_level[1:], axis=1)
        gathered = stacked[:, pattern - 2, :]
        couplings = coupling_rows.astype(jnp.float32).reshape(LNODES, RANK, COUP, RANK)
        local_terms = jnp.einsum("nicj,rncj->rni", couplings, gathered, precision=highest)
        current = field_root[:, None, :]
        for level_now in range(LOCAL_LEVELS):
            groups = 2 ** level_now
            from_above = jnp.einsum("picj,rpj->rpci", pairings[groups - 1:2 * groups - 1], current, precision=highest).reshape(NRHS, 2 * groups, RANK)
            current = local_terms[:, 2 * groups - 2:4 * groups - 2, :] + from_above
        leaf_basis = basis_rows.reshape(LEAVES_DEV, LEAF, RANK).astype(jnp.float32)
        far_part = jnp.einsum("lpk,rlk->rlp", leaf_basis, current, precision=highest)
        window = lax.dynamic_slice_in_dim(padded, (index_now * LEAVES_DEV).astype(jnp.int32), LEAVES_DEV + 2 * RANGE, 1)
        chosen = jnp.arange(LEAVES_DEV, dtype=jnp.int32)[:, None] + RANGE + offsets
        partners = window[:, chosen, :].reshape(NRHS, LEAVES_DEV, NEAR * LEAF)
        near_part = jnp.einsum("lpq,rlq->rlp", blocks.astype(jnp.float32), partners.astype(jnp.float32), precision=highest)
        combined = (near_part + far_part).reshape(NRHS, PTS_DEV)
        return jnp.zeros_like(combined).at[:, order_here].set(combined)

    results = lax.map(finish, (
        jnp.arange(devices, dtype=jnp.int32),
        clustered,
        basis_all,
        pairing_all,
        near_offsets.reshape(devices, LEAVES_DEV, NEAR),
        near_blocks.reshape(devices, LEAVES_DEV, LEAF, NEAR * LEAF),
        coupling_pattern.reshape(devices, LNODES, COUP),
        local_coupling.reshape(devices, LNODES, RANK, COUP * RANK),
        fields_root,
        cluster_perm,
    ))
    return results.transpose(1, 0, 2).reshape(NRHS, POINTS)
```

```python
import jax
import jax.numpy as jnp
from jax import lax
from jax.experimental import pallas as pl
from jax.experimental.pallas import tpu as pltpu
from jax.sharding import PartitionSpec as P

F32 = jnp.float32
BF16 = jnp.bfloat16
MESH = pl.DeviceIdType.MESH
NRHS = 16
RANK = 64
LEAVES = 64
POINTS = 4096
SPAN = 256
CHUNKS = POINTS // SPAN
COARSE = POINTS // SPAN

TOP_ROWS = [(7, 0), (7, 1), (7, 2), (7, 3), (6, 0), (6, 1), (5, 0)]
TOP_ROWS += [(4, 0), (4, 1), (4, 2), (4, 3), (3, 0), (3, 1), (2, 0), (1, 0), (0, 0)]
TOP_SLOT = {row: slot for slot, row in enumerate(TOP_ROWS)}


def nn(a, b):
    return lax.dot_general(a, b, (((1,), (0,)), ((), ())), preferred_element_type=F32)


def nt(a, b):
    return lax.dot_general(a, b, (((1,), (1,)), ((), ())), preferred_element_type=F32)


def flipped(index, mask):
    out = index
    for bit in range(8):
        if (mask >> bit) & 1:
            step = 1 << bit
            out = out + step * (1 - 2 * lax.rem(lax.div(index, step), 2))
    return out


def split(x):
    high = x.astype(BF16)
    return high, (x - high.astype(F32)).astype(BF16)


def stacked(x):
    return jnp.concatenate(split(x), axis=0)[:, :RANK]


def folded(x):
    return x[0:NRHS] + x[NRHS : 2 * NRHS]


def swapped(x):
    return pltpu.roll(x, RANK, axis=1)


def kernel(
    offsets,
    pattern,
    measured_hbm,
    perm_hbm,
    near_hbm,
    bases_hbm,
    transfer_hbm,
    coupling_hbm,
    root_hbm,
    top_hbm,
    out,
    measured,
    perm,
    near_blocks,
    bases,
    transfer,
    coupling,
    root_row,
    tops,
    tops_swapped,
    root_wide,
    basis_wide,
    basis,
    onehot,
    points,
    coef,
    local_terms,
    near_part,
    fields,
    combined,
    edges,
    halo,
    first,
    second,
    third,
    in_sem,
    top_sem,
    halo_send,
    halo_recv,
    first_send,
    first_recv,
    second_send,
    second_recv,
    third_send,
    third_recv,
):
    me = lax.axis_index("leaf")
    right = lax.rem(me + 1, 256)
    left = lax.rem(me + 255, 256)
    low = lax.broadcasted_iota(jnp.int32, (NRHS, 128), 1) < RANK

    loads = [
        pltpu.make_async_copy(source, target, in_sem.at[i])
        for i, (source, target) in enumerate(
            [
                (perm_hbm, perm),
                (measured_hbm, measured),
                (bases_hbm, bases),
                (root_hbm, root_row),
                (transfer_hbm, transfer),
                (coupling_hbm, coupling),
                (near_hbm, near_blocks),
            ]
        )
    ]
    for load in loads[:5]:
        load.start()
    top_loads = []
    for slot, (level, relative) in enumerate(TOP_ROWS):
        node = (1 << level) + flipped(lax.div(me, 1 << (8 - level)), relative)
        top_loads.append(pltpu.make_async_copy(top_hbm.at[node], tops.at[slot], top_sem.at[slot]))
        top_loads[-1].start()
    for load in loads[5:]:
        load.start()

    barrier = pltpu.get_barrier_semaphore()
    peers = [flipped(me, k) for k in range(1, 8)]
    peers += [flipped(me, 8 * k) for k in range(1, 8)]
    peers += [flipped(me, 64 * k) for k in range(1, 4)]
    peers += [left, right]
    for peer in peers:
        pl.semaphore_signal(barrier, inc=1, device_id=(peer,), device_id_type=MESH)

    loads[0].wait()
    loads[1].wait()
    spread = jnp.concatenate(
        [measured[:, h * SPAN : (h + 1) * SPAN] for h in range(COARSE)], axis=0
    )
    rows = lax.broadcasted_iota(jnp.int32, (SPAN, SPAN), 0)
    for c in range(CHUNKS):
        at = slice(c * SPAN, (c + 1) * SPAN)
        order = perm[0:1, at]
        hot = jnp.where(rows == lax.rem(order, SPAN), 1.0, 0.0).astype(BF16)
        onehot[:, at] = hot
        picked = nn(spread, hot)
        coarse = jnp.broadcast_to(lax.div(order, SPAN), (NRHS, SPAN))
        chosen = picked[0:NRHS]
        for h in range(1, COARSE):
            chosen = jnp.where(coarse == h, picked[h * NRHS : (h + 1) * NRHS], chosen)
        for pair in range(2):
            both = chosen[:, pair * 128 : (pair + 1) * 128]
            turned = swapped(both)
            leaf = 4 * c + 2 * pair
            points[leaf + 2] = jnp.where(low, both, turned).astype(BF16)
            points[leaf + 3] = jnp.where(low, turned, both).astype(BF16)
            if leaf == 0:
                edges[0] = both.astype(BF16)
            if leaf == LEAVES - 2:
                edges[1] = both.astype(BF16)

    pl.semaphore_wait(barrier, len(peers))
    halo_copies = [
        pltpu.make_async_remote_copy(
            src_ref=edges.at[side],
            dst_ref=halo.at[side],
            send_sem=halo_send.at[side],
            recv_sem=halo_recv.at[side],
            device_id=(target,),
            device_id_type=MESH,
        )
        for side, target in ((0, left), (1, right))
    ]
    for copy in halo_copies:
        copy.start()

    loads[2].wait()
    low_leaves = lax.broadcasted_iota(jnp.int32, (LEAVES, 128), 1) < RANK
    for pair in range(32):
        both = bases[:, pair * 128 : (pair + 1) * 128].astype(F32)
        turned = swapped(both)
        basis_wide[pl.ds(2 * pair, LEAVES, stride=RANK), :] = jnp.where(low_leaves, both, turned)
        basis_wide[pl.ds(2 * pair + 1, LEAVES, stride=RANK), :] = jnp.where(low_leaves, turned, both)
    basis[...] = basis_wide[...].astype(BF16)

    loads[3].wait()
    low_row = lax.broadcasted_iota(jnp.int32, (1, 128), 1) < RANK
    for pair in range(32):
        both = root_row[0:1, pair * 128 : (pair + 1) * 128].astype(F32)
        turned = swapped(both)
        root_wide[2 * pair : 2 * pair + 1, :] = jnp.where(low_row, both, turned)
        root_wide[2 * pair + 1 : 2 * pair + 2, :] = jnp.where(low_row, turned, both)
    root_map = root_wide[...].astype(BF16)

    quarter = lax.broadcasted_iota(jnp.int32, (NRHS, 256), 1) // RANK
    for four in range(LEAVES // 4):
        lanes = [points[2 + 4 * four + k].astype(F32) for k in range(4)]
        wide = [
            jnp.concatenate([lanes[k], lanes[k]], axis=1) for k in range(4)
        ]
        block = jnp.concatenate(
            [jnp.where(quarter == k, wide[k], 0.0) for k in range(4)], axis=0
        ).astype(BF16)
        result = nn(block, basis[four * 256 : (four + 1) * 256, :])
        for k in range(4):
            coef[64 + 4 * four + k] = jnp.concatenate(
                split(result[k * NRHS : (k + 1) * NRHS]), axis=0
            )

    loads[4].wait()

    def climb(parent):
        children = coef[pl.ds(2 * parent, 2)].reshape(64, 128)[:, :RANK]
        result = nn(children, transfer[parent - 1])
        mixed = jnp.where(low, folded(result[0:32]), folded(result[32:64]))
        return mixed + swapped(mixed)

    for level in range(5, 0, -1):
        groups = 1 << level
        for parent in range(groups, 2 * groups):
            coef[parent] = jnp.concatenate(split(climb(parent)), axis=0)
    root_coef = climb(1)
    root_up = folded(nn(stacked(root_coef), root_map))
    first[0] = jnp.where(low, root_up, root_coef)

    def exchange(buffer, count, shift, send_sem, recv_sem):
        copies = [
            pltpu.make_async_remote_copy(
                src_ref=buffer.at[0],
                dst_ref=buffer.at[k],
                send_sem=send_sem.at[k],
                recv_sem=recv_sem.at[k],
                device_id=(flipped(me, k << shift),),
                device_id_type=MESH,
            )
            for k in range(1, count)
        ]
        for copy in copies:
            copy.start()
        return copies

    first_copies = exchange(first, 8, 0, first_send, first_recv)

    for load in top_loads:
        load.wait()
    for slot in range(len(TOP_ROWS)):
        tops_swapped[slot] = swapped(tops[slot].astype(F32)).astype(BF16)

    loads[5].wait()

    def couple(pair):
        sides = []
        for k in range(2):
            n = 2 * pair + k
            sides.append(
                jnp.concatenate(
                    [coef[pattern[0, n]][:, :RANK], coef[pattern[1, n]][:, RANK:]], axis=1
                )
            )
        blocks = coupling[pl.ds(2 * pair, 2)].reshape(128, 128)
        result = nt(jnp.concatenate(sides, axis=0), blocks)
        local_terms[pair + 1] = jnp.where(low, folded(result[0:32]), folded(result[32:64]))

    def near(pair):
        sides = []
        for k in range(2):
            leaf = 2 * pair + k
            at = [points[leaf + 2 + offsets[j, leaf]] for j in range(4)]
            sides.append(
                jnp.concatenate(
                    [at[0][:, :RANK], at[1][:, RANK:], at[2][:, :RANK], at[3][:, RANK:]], axis=1
                )
            )
        blocks = near_blocks[pl.ds(2 * pair, 2)].reshape(128, 256)
        result = nt(jnp.concatenate(sides, axis=0), blocks)
        near_part[pair] = jnp.where(low, result[0:NRHS], result[NRHS : 2 * NRHS])

    @pl.loop(0, 9)
    def _(step):
        for k in range(7):
            couple(7 * step + k)

    def lift(values, level):
        return [
            folded(nn(stacked(value), tops_swapped[TOP_SLOT[level, k]]))
            for k, value in enumerate(values)
        ]

    def added(values):
        return [values[2 * k] + values[2 * k + 1] for k in range(len(values) // 2)]

    def coupled(sibling, level):
        block = tops[TOP_SLOT[level - 1, 0]]
        parts = stacked(sibling)
        to_left = folded(nt(parts, block[:, :RANK]))
        to_right = folded(nn(parts, block))[:, :RANK]
        odd = lax.rem(lax.div(me, 1 << (8 - level)), 2)
        return jnp.where(odd == 1, to_right, to_left)

    terms = {}
    for copy in first_copies:
        copy.wait()
    at_7 = added([first[k] for k in range(8)])
    at_6 = added(lift(at_7, 7))
    at_5 = added(lift(at_6, 6))[0]
    second[0] = jnp.where(low, lift([at_5], 5)[0], swapped(at_5))
    second_copies = exchange(second, 8, 3, second_send, second_recv)
    terms[8] = coupled(swapped(first[1]), 8)
    terms[7] = coupled(at_7[1], 7)
    terms[6] = coupled(at_6[1], 6)

    for copy in halo_copies:
        copy.wait()
    for side, leaf, end in ((1, 0, 0), (0, 66, 255)):
        both = jnp.where(me == end, 0.0, halo[side].astype(F32))
        turned = swapped(both)
        points[leaf] = jnp.where(low, both, turned).astype(BF16)
        points[leaf + 1] = jnp.where(low, turned, both).astype(BF16)
    loads[6].wait()

    @pl.loop(0, 4)
    def _(step):
        for k in range(8):
            near(8 * step + k)

    for copy in second_copies:
        copy.wait()
    at_4 = added([second[k] for k in range(8)])
    at_3 = added(lift(at_4, 4))
    at_2 = added(lift(at_3, 3))[0]
    third[0] = jnp.where(low, lift([at_2], 2)[0], swapped(at_2))
    third_copies = exchange(third, 4, 6, third_send, third_recv)
    terms[5] = coupled(swapped(second[1]), 5)
    terms[4] = coupled(at_4[1], 4)
    terms[3] = coupled(at_3[1], 3)

    for copy in third_copies:
        copy.wait()
    at_1 = added([third[k] for k in range(4)])
    terms[2] = coupled(swapped(third[1]), 2)
    terms[1] = coupled(at_1[1], 1)
    field = terms[1]
    for level in range(2, 8):
        block = tops_swapped[TOP_SLOT[level, 0]][:, :RANK]
        field = terms[level] + folded(nt(stacked(field), block))
    field = terms[8] + folded(nt(stacked(field), root_map[:, :RANK]))

    def descend(parent, here, there):
        lhs = jnp.concatenate(
            [jnp.where(low, part, 0.0) for part in here]
            + [jnp.where(low, 0.0, part) for part in there],
            axis=0,
        ).astype(BF16)
        block = transfer[parent - 1]
        result = nt(lhs, jnp.concatenate([block, block], axis=0))
        fields[parent] = local_terms[parent] + jnp.where(
            low, folded(result[0:32]), folded(result[32:64])
        )

    def parts_of(x):
        high = x.astype(BF16).astype(F32)
        return high, x - high

    root_parts = parts_of(jnp.concatenate([field, field], axis=1))
    descend(1, root_parts, root_parts)
    for level in range(5):
        for q in range(1 << level, 2 << level):
            pair = fields[q]
            straight = parts_of(pair)
            crossed = parts_of(swapped(pair))
            descend(2 * q, straight, crossed)
            descend(2 * q + 1, crossed, straight)

    for m in range(32):
        pair = fields[32 + m]
        lhs = jnp.concatenate(split(pair) + split(swapped(pair)), axis=0)[:, :RANK]
        result = nt(lhs, basis[m * 128 : (m + 1) * 128, :RANK])
        whole = near_part[m] + jnp.where(low, folded(result[0:32]), folded(result[32:64]))
        combined[:, m * 128 : (m + 1) * 128] = jnp.concatenate(parts_of(whole), axis=0)

    total = jnp.zeros((COARSE * 32, SPAN), F32)
    for c in range(CHUNKS):
        at = slice(c * SPAN, (c + 1) * SPAN)
        coarse = jnp.broadcast_to(lax.div(perm[0:1, at], SPAN), (32, SPAN))
        values = combined[:, at]
        lhs = jnp.concatenate(
            [jnp.where(coarse == h, values, 0.0) for h in range(COARSE)], axis=0
        ).astype(BF16)
        total = total + nt(lhs, onehot[:, at])
    for h in range(COARSE):
        out[:, h * SPAN : (h + 1) * SPAN] = folded(total[h * 32 : (h + 1) * 32])


def body(
    measured,
    cluster_perm,
    near_offsets,
    near_blocks,
    leaf_bases,
    local_transfer,
    coupling_pattern,
    local_coupling,
    root_transfer,
    top_blocks,
):
    smem = pl.BlockSpec(memory_space=pltpu.SMEM)
    hbm = pl.BlockSpec(memory_space=pl.ANY)
    dma = pltpu.SemaphoreType.DMA
    return pl.pallas_call(
        kernel,
        out_shape=jax.ShapeDtypeStruct((NRHS, POINTS), F32),
        in_specs=[smem, smem] + [hbm] * 8,
        out_specs=pl.BlockSpec(memory_space=pltpu.VMEM),
        scratch_shapes=[
            pltpu.VMEM((NRHS, POINTS), BF16),
            pltpu.VMEM((1, POINTS), jnp.int32),
            pltpu.VMEM((64, 64, 256), BF16),
            pltpu.VMEM((64, 4096), BF16),
            pltpu.VMEM((63, 64, 128), BF16),
            pltpu.VMEM((126, 64, 128), BF16),
            pltpu.VMEM((1, 4096), BF16),
            pltpu.VMEM((16, 64, 128), BF16),
            pltpu.VMEM((16, 64, 128), BF16),
            pltpu.VMEM((64, 128), F32),
            pltpu.VMEM((4096, 128), F32),
            pltpu.VMEM((4096, 128), BF16),
            pltpu.VMEM((SPAN, POINTS), BF16),
            pltpu.VMEM((68, NRHS, 128), BF16),
            pltpu.VMEM((128, 2 * NRHS, 128), BF16),
            pltpu.VMEM((64, NRHS, 128), F32),
            pltpu.VMEM((32, NRHS, 128), F32),
            pltpu.VMEM((64, NRHS, 128), F32),
            pltpu.VMEM((2 * NRHS, POINTS), F32),
            pltpu.VMEM((2, NRHS, 128), BF16),
            pltpu.VMEM((2, NRHS, 128), BF16),
            pltpu.VMEM((8, NRHS, 128), F32),
            pltpu.VMEM((8, NRHS, 128), F32),
            pltpu.VMEM((4, NRHS, 128), F32),
            dma((7,)),
            dma((16,)),
            dma((2,)),
            dma((2,)),
            dma((8,)),
            dma((8,)),
            dma((8,)),
            dma((8,)),
            dma((4,)),
            dma((4,)),
        ],
        compiler_params=pltpu.CompilerParams(
            collective_id=0, has_side_effects=True, vmem_limit_bytes=40 * 1024 * 1024
        ),
    )(
        near_offsets.T,
        coupling_pattern.T,
        measured,
        cluster_perm,
        near_blocks,
        leaf_bases,
        local_transfer,
        local_coupling,
        root_transfer,
        top_blocks,
    )


def solution(mesh):
    return jax.shard_map(
        body,
        mesh=mesh,
        in_specs=(
            P(None, "leaf"),
            P("leaf", None),
            P("leaf", None),
            P("leaf", None, None),
            P("leaf", None),
            P("leaf", None, None),
            P("leaf", None),
            P("leaf", None, None),
            P("leaf", None),
            P(),
        ),
        out_specs=P(None, "leaf"),
        check_vma=False,
    )
```

```python
import jax
import jax.numpy as jnp
from jax import lax
from jax.experimental import pallas as pl
from jax.experimental.pallas import tpu as pltpu
from jax.sharding import PartitionSpec as P

F32 = jnp.float32
BF16 = jnp.bfloat16
MESH = pl.DeviceIdType.MESH
NRHS = 16
RANK = 64
LEAVES = 64
POINTS = 4096
SPAN = 256
CHUNKS = POINTS // SPAN
COARSE = POINTS // SPAN

UP_SLOT = {4: 0, 3: 16, 2: 24, 7: 28, 6: 32, 5: 34}
UP_COUNT = {4: 16, 3: 8, 2: 4, 7: 4, 6: 2, 5: 1}

NEAR_PEERS = (4, 5, 6, 7, 2, 3, 1)
Z_HOPS = (0, 1, 2, 3, 4, 3, 2, 3)
Y_HOPS = (0, 1, 2, 1)
FAR_PEERS = tuple(sorted(range(1, 32), key=lambda k: -Z_HOPS[k % 8] - Y_HOPS[k // 8]))


def nn(a, b):
    return lax.dot_general(a, b, (((1,), (0,)), ((), ())), preferred_element_type=F32)


def nt(a, b):
    return lax.dot_general(a, b, (((1,), (1,)), ((), ())), preferred_element_type=F32)


def flipped(index, mask):
    out = index
    for bit in range(8):
        if (mask >> bit) & 1:
            step = 1 << bit
            out = out + step * (1 - 2 * lax.rem(lax.div(index, step), 2))
    return out


def split(x):
    high = x.astype(BF16)
    return high, (x - high.astype(F32)).astype(BF16)


def stacked(x):
    return jnp.concatenate(split(x), axis=0)[:, :RANK]


def folded(x):
    return x[0:NRHS] + x[NRHS : 2 * NRHS]


def swapped(x):
    return pltpu.roll(x, RANK, axis=1)


def kernel(
    offsets_hbm,
    pattern_hbm,
    measured_hbm,
    perm_hbm,
    near_hbm,
    bases_hbm,
    transfer_hbm,
    coupling_hbm,
    root_hbm,
    top_hbm,
    out,
    offsets,
    pattern,
    measured,
    perm,
    near_blocks,
    bases,
    transfer,
    coupling,
    root_row,
    tops,
    climbs,
    root_wide,
    basis_wide,
    basis,
    onehot,
    points,
    coef,
    local_terms,
    near_part,
    fields,
    combined,
    edges,
    halo,
    first,
    first_coef,
    second,
    second_coef,
    in_sem,
    top_sem,
    send_sem,
    recv_sem,
):
    me = lax.axis_index("leaf")
    right = lax.rem(me + 1, 256)
    left = lax.rem(me + 255, 256)
    low = lax.broadcasted_iota(jnp.int32, (NRHS, 128), 1) < RANK

    loads = [
        pltpu.make_async_copy(source, target, in_sem.at[i])
        for i, (source, target) in enumerate(
            [
                (perm_hbm, perm),
                (measured_hbm, measured),
                (bases_hbm, bases),
                (root_hbm, root_row),
                (transfer_hbm, transfer),
                (coupling_hbm, coupling),
                (near_hbm, near_blocks),
                (pattern_hbm, pattern),
                (offsets_hbm, offsets),
            ]
        )
    ]
    for load in loads[:2]:
        load.start()

    barrier = pltpu.get_barrier_semaphore()
    peers = [flipped(me, 8 * k) for k in FAR_PEERS] + [left, right]
    peers += [flipped(me, k) for k in NEAR_PEERS]
    for peer in peers:
        pl.semaphore_signal(barrier, inc=1, device_id=(peer,), device_id_type=MESH)

    for load in loads[2:5]:
        load.start()
    group = lax.div(me, 8)
    top_loads = [
        pltpu.make_async_copy(top_hbm.at[pl.ds(start, count)], tops.at[pl.ds(at, count)], top_sem.at[0])
        for start, at, count in (
            (0, 0, 32),
            (32 + group, 32, 1),
            (64 + 2 * group, 33, 2),
            (128 + 4 * group, 35, 4),
        )
    ]
    for load in top_loads:
        load.start()
    for load in loads[5:]:
        load.start()

    loads[0].wait()
    loads[1].wait()
    spread = jnp.concatenate(
        [measured[:, h * SPAN : (h + 1) * SPAN] for h in range(COARSE)], axis=0
    )
    rows = lax.broadcasted_iota(jnp.int32, (SPAN, SPAN), 0)
    for c in range(CHUNKS):
        at = slice(c * SPAN, (c + 1) * SPAN)
        order = perm[0:1, at]
        hot = jnp.where(rows == lax.rem(order, SPAN), 1.0, 0.0).astype(BF16)
        onehot[:, at] = hot
        picked = nn(spread, hot)
        coarse = jnp.broadcast_to(lax.div(order, SPAN), (NRHS, SPAN))
        chosen = picked[0:NRHS]
        for h in range(1, COARSE):
            chosen = jnp.where(coarse == h, picked[h * NRHS : (h + 1) * NRHS], chosen)
        for pair in range(2):
            both = chosen[:, pair * 128 : (pair + 1) * 128]
            turned = swapped(both)
            leaf = 4 * c + 2 * pair
            points[leaf + 2] = jnp.where(low, both, turned).astype(BF16)
            points[leaf + 3] = jnp.where(low, turned, both).astype(BF16)
            if leaf == 0:
                edges[0] = both.astype(BF16)
            if leaf == LEAVES - 2:
                edges[1] = both.astype(BF16)

    loads[2].wait()
    low_leaves = lax.broadcasted_iota(jnp.int32, (LEAVES, 128), 1) < RANK
    for pair in range(32):
        both = bases[:, pair * 128 : (pair + 1) * 128].astype(F32)
        turned = swapped(both)
        basis_wide[pl.ds(2 * pair, LEAVES, stride=RANK), :] = jnp.where(low_leaves, both, turned)
        basis_wide[pl.ds(2 * pair + 1, LEAVES, stride=RANK), :] = jnp.where(low_leaves, turned, both)
    basis[...] = basis_wide[...].astype(BF16)

    loads[3].wait()
    low_row = lax.broadcasted_iota(jnp.int32, (1, 128), 1) < RANK
    for pair in range(32):
        both = root_row[0:1, pair * 128 : (pair + 1) * 128].astype(F32)
        turned = swapped(both)
        root_wide[2 * pair : 2 * pair + 1, :] = jnp.where(low_row, both, turned)
        root_wide[2 * pair + 1 : 2 * pair + 2, :] = jnp.where(low_row, turned, both)
    root_map = root_wide[...].astype(BF16)

    quarter = lax.broadcasted_iota(jnp.int32, (NRHS, 256), 1) // RANK
    for four in range(LEAVES // 4):
        lanes = [points[2 + 4 * four + k].astype(F32) for k in range(4)]
        wide = [
            jnp.concatenate([lanes[k], lanes[k]], axis=1) for k in range(4)
        ]
        block = jnp.concatenate(
            [jnp.where(quarter == k, wide[k], 0.0) for k in range(4)], axis=0
        ).astype(BF16)
        result = nn(block, basis[four * 256 : (four + 1) * 256, :])
        for k in range(4):
            coef[64 + 4 * four + k] = jnp.concatenate(
                split(result[k * NRHS : (k + 1) * NRHS]), axis=0
            )

    loads[4].wait()

    def climb(parent):
        children = coef[pl.ds(2 * parent, 2)].reshape(64, 128)[:, :RANK]
        result = nn(children, transfer[parent - 1])
        mixed = jnp.where(low, folded(result[0:32]), folded(result[32:64]))
        return mixed + swapped(mixed)

    for level in range(5, 0, -1):
        groups = 1 << level
        for parent in range(groups, 2 * groups):
            coef[parent] = jnp.concatenate(split(climb(parent)), axis=0)
    root_coef = climb(1)
    root_up = folded(nn(stacked(root_coef), root_map))

    def packed(x):
        high = x.astype(BF16).astype(F32)
        return jnp.where(low, high, x - high).astype(BF16)

    def opened(x):
        return x + swapped(x)

    def send(buffer, slot, mask, at):
        copy = pltpu.make_async_remote_copy(
            src_ref=buffer.at[0],
            dst_ref=buffer.at[slot],
            send_sem=send_sem.at[at],
            recv_sem=recv_sem.at[at],
            device_id=(flipped(me, mask),),
            device_id_type=MESH,
        )
        copy.start()

    def arrived(buffer, at):
        slots = buffer.at[pl.ds(1, buffer.shape[0] - 1)]
        pltpu.make_async_remote_copy(
            src_ref=slots,
            dst_ref=slots,
            send_sem=send_sem.at[at],
            recv_sem=recv_sem.at[at],
            device_id=(flipped(me, 1),),
            device_id_type=MESH,
        ).wait()

    first[0] = packed(root_up)
    first_coef[0] = packed(root_coef)
    pl.semaphore_wait(barrier, len(peers))
    for k in NEAR_PEERS:
        send(first, k, k, 0)
    send(first_coef, 1, 1, 1)
    halo_copies = [
        pltpu.make_async_remote_copy(
            src_ref=edges.at[side],
            dst_ref=halo.at[side],
            send_sem=send_sem.at[4],
            recv_sem=recv_sem.at[4],
            device_id=(target,),
            device_id_type=MESH,
        )
        for side, target in ((0, left), (1, right))
    ]
    for copy in halo_copies:
        copy.start()

    pltpu.make_async_copy(top_hbm.at[pl.ds(0, 39)], tops, top_sem.at[0]).wait()
    low_rank = lax.broadcasted_iota(jnp.int32, (RANK, 128), 1) < RANK

    def top_row(level, k):
        if level == 0:
            return 1
        own = lax.div(me, 1 << (8 - level))
        if level < 5:
            return (1 << level) + flipped(own, k)
        if level == 5:
            return 32
        return (33 if level == 6 else 35) + flipped(lax.rem(own, 1 << (level - 5)), k)

    for level, count in UP_COUNT.items():
        for k in range(count):
            block = tops[top_row(level, k)].astype(F32)
            climbs[UP_SLOT[level] + k] = jnp.where(low_rank, swapped(block), block).astype(BF16)

    loads[5].wait()
    loads[7].wait()

    def couple(pair):
        sides = []
        for k in range(2):
            n = 2 * pair + k
            sides.append(
                jnp.concatenate(
                    [coef[pattern[0, n]][:, :RANK], coef[pattern[1, n]][:, RANK:]], axis=1
                )
            )
        blocks = coupling[pl.ds(2 * pair, 2)].reshape(128, 128)
        result = nt(jnp.concatenate(sides, axis=0), blocks)
        local_terms[pair + 1] = jnp.where(low, folded(result[0:32]), folded(result[32:64]))

    def near(pair):
        sides = []
        for k in range(2):
            leaf = 2 * pair + k
            at = [points[leaf + 2 + offsets[j, leaf]] for j in range(4)]
            sides.append(
                jnp.concatenate(
                    [at[0][:, :RANK], at[1][:, RANK:], at[2][:, :RANK], at[3][:, RANK:]], axis=1
                )
            )
        blocks = near_blocks[pl.ds(2 * pair, 2)].reshape(128, 256)
        result = nt(jnp.concatenate(sides, axis=0), blocks)
        near_part[pair] = jnp.where(low, result[0:NRHS], result[NRHS : 2 * NRHS])

    @pl.loop(0, 9)
    def _(step):
        for k in range(7):
            couple(7 * step + k)

    def lift(values, level):
        out = []
        for k in range(0, len(values), 2):
            both = jnp.where(low, values[k], values[k + 1])
            blocks = climbs[pl.ds(UP_SLOT[level] + k, 2)].reshape(128, 128)
            out.append(folded(nn(jnp.concatenate(split(both), axis=0), blocks)))
        return out

    def coupled(sibling, level):
        block = tops[top_row(level - 1, 0)]
        parts = stacked(sibling)
        to_left = folded(nt(parts, block[:, :RANK]))
        to_right = folded(nn(parts, block))[:, :RANK]
        odd = lax.rem(lax.div(me, 1 << (8 - level)), 2)
        return jnp.where(odd == 1, to_right, to_left)

    def received(buffer, k):
        return opened(buffer[k].astype(F32) + buffer[k + 1].astype(F32))

    terms = {}
    arrived(first, 0)
    arrived(first_coef, 1)
    at_7 = [received(first, 2 * k) for k in range(4)]
    at_6 = lift(at_7, 7)
    at_5 = lift(at_6, 6)[0]
    second[0] = packed(folded(nn(stacked(at_5), climbs[UP_SLOT[5]])))
    second_coef[0] = packed(at_5)
    for k in FAR_PEERS:
        send(second, k, 8 * k, 2)
    send(second_coef, 1, 8, 3)
    terms[8] = coupled(opened(first_coef[1].astype(F32)), 8)
    terms[7] = coupled(at_7[1], 7)
    terms[6] = coupled(at_6[1], 6)

    pltpu.make_async_remote_copy(
        src_ref=edges,
        dst_ref=halo,
        send_sem=send_sem.at[4],
        recv_sem=recv_sem.at[4],
        device_id=(left,),
        device_id_type=MESH,
    ).wait()
    for side, leaf, end in ((1, 0, 0), (0, 66, 255)):
        both = jnp.where(me == end, 0.0, halo[side].astype(F32))
        turned = swapped(both)
        points[leaf] = jnp.where(low, both, turned).astype(BF16)
        points[leaf + 1] = jnp.where(low, turned, both).astype(BF16)
    loads[6].wait()
    loads[8].wait()

    @pl.loop(0, 4)
    def _(step):
        for k in range(8):
            near(8 * step + k)

    arrived(second, 2)
    arrived(second_coef, 3)
    at_4 = [received(second, 2 * k) for k in range(16)]
    at_3 = lift(at_4, 4)
    at_2 = lift(at_3, 3)
    at_1 = lift(at_2, 2)
    terms[5] = coupled(opened(second_coef[1].astype(F32)), 5)
    terms[4] = coupled(at_4[1], 4)
    terms[3] = coupled(at_3[1], 3)
    terms[2] = coupled(at_2[1], 2)
    terms[1] = coupled(at_1[1], 1)
    field = terms[1]
    for level in range(2, 8):
        block = climbs[UP_SLOT[level]][:, :RANK]
        field = terms[level] + folded(nt(stacked(field), block))
    field = terms[8] + folded(nt(stacked(field), root_map[:, :RANK]))

    def descend(parent, here, there):
        lhs = jnp.concatenate(
            [jnp.where(low, part, 0.0) for part in here]
            + [jnp.where(low, 0.0, part) for part in there],
            axis=0,
        ).astype(BF16)
        block = transfer[parent - 1]
        result = nt(lhs, jnp.concatenate([block, block], axis=0))
        fields[parent] = local_terms[parent] + jnp.where(
            low, folded(result[0:32]), folded(result[32:64])
        )

    def parts_of(x):
        high = x.astype(BF16).astype(F32)
        return high, x - high

    root_parts = parts_of(jnp.concatenate([field, field], axis=1))
    descend(1, root_parts, root_parts)
    for level in range(5):
        for q in range(1 << level, 2 << level):
            pair = fields[q]
            straight = parts_of(pair)
            crossed = parts_of(swapped(pair))
            descend(2 * q, straight, crossed)
            descend(2 * q + 1, crossed, straight)

    for m in range(32):
        pair = fields[32 + m]
        lhs = jnp.concatenate(split(pair) + split(swapped(pair)), axis=0)[:, :RANK]
        result = nt(lhs, basis[m * 128 : (m + 1) * 128, :RANK])
        whole = near_part[m] + jnp.where(low, folded(result[0:32]), folded(result[32:64]))
        combined[:, m * 128 : (m + 1) * 128] = jnp.concatenate(parts_of(whole), axis=0)

    total = jnp.zeros((COARSE * 32, SPAN), F32)
    for c in range(CHUNKS):
        at = slice(c * SPAN, (c + 1) * SPAN)
        coarse = jnp.broadcast_to(lax.div(perm[0:1, at], SPAN), (32, SPAN))
        values = combined[:, at]
        lhs = jnp.concatenate(
            [jnp.where(coarse == h, values, 0.0) for h in range(COARSE)], axis=0
        ).astype(BF16)
        total = total + nt(lhs, onehot[:, at])
    for h in range(COARSE):
        out[:, h * SPAN : (h + 1) * SPAN] = folded(total[h * 32 : (h + 1) * 32])


def body(
    measured,
    cluster_perm,
    near_offsets,
    near_blocks,
    leaf_bases,
    local_transfer,
    coupling_pattern,
    local_coupling,
    root_transfer,
    top_blocks,
):
    hbm = pl.BlockSpec(memory_space=pl.ANY)
    dma = pltpu.SemaphoreType.DMA
    return pl.pallas_call(
        kernel,
        out_shape=jax.ShapeDtypeStruct((NRHS, POINTS), F32),
        in_specs=[hbm] * 10,
        out_specs=pl.BlockSpec(memory_space=pltpu.VMEM),
        scratch_shapes=[
            pltpu.SMEM((4, 64), jnp.int32),
            pltpu.SMEM((2, 126), jnp.int32),
            pltpu.VMEM((NRHS, POINTS), BF16),
            pltpu.VMEM((1, POINTS), jnp.int32),
            pltpu.VMEM((64, 64, 256), BF16),
            pltpu.VMEM((64, 4096), BF16),
            pltpu.VMEM((63, 64, 128), BF16),
            pltpu.VMEM((126, 64, 128), BF16),
            pltpu.VMEM((1, 4096), BF16),
            pltpu.VMEM((39, 64, 128), BF16),
            pltpu.VMEM((35, 64, 128), BF16),
            pltpu.VMEM((64, 128), F32),
            pltpu.VMEM((4096, 128), F32),
            pltpu.VMEM((4096, 128), BF16),
            pltpu.VMEM((SPAN, POINTS), BF16),
            pltpu.VMEM((68, NRHS, 128), BF16),
            pltpu.VMEM((128, 2 * NRHS, 128), BF16),
            pltpu.VMEM((64, NRHS, 128), F32),
            pltpu.VMEM((32, NRHS, 128), F32),
            pltpu.VMEM((64, NRHS, 128), F32),
            pltpu.VMEM((2 * NRHS, POINTS), F32),
            pltpu.VMEM((2, NRHS, 128), BF16),
            pltpu.VMEM((2, NRHS, 128), BF16),
            pltpu.VMEM((8, NRHS, 128), BF16),
            pltpu.VMEM((2, NRHS, 128), BF16),
            pltpu.VMEM((32, NRHS, 128), BF16),
            pltpu.VMEM((2, NRHS, 128), BF16),
            dma((9,)),
            dma((1,)),
            dma((5,)),
            dma((5,)),
        ],
        compiler_params=pltpu.CompilerParams(
            collective_id=0, has_side_effects=True, vmem_limit_bytes=62 * 1024 * 1024
        ),
    )(
        near_offsets.T,
        coupling_pattern.T,
        measured,
        cluster_perm,
        near_blocks,
        leaf_bases,
        local_transfer,
        local_coupling,
        root_transfer,
        top_blocks,
    )


def solution(mesh):
    return jax.shard_map(
        body,
        mesh=mesh,
        in_specs=(
            P(None, "leaf"),
            P("leaf", None),
            P("leaf", None),
            P("leaf", None, None),
            P("leaf", None),
            P("leaf", None, None),
            P("leaf", None),
            P("leaf", None, None),
            P("leaf", None),
            P(),
        ),
        out_specs=P(None, "leaf"),
        check_vma=False,
    )
```

```python
import jax
import jax.numpy as jnp
from jax import lax
from jax.experimental import pallas as pl
from jax.experimental.pallas import tpu as pltpu
from jax.sharding import PartitionSpec as P

F32 = jnp.float32
BF16 = jnp.bfloat16
MESH = pl.DeviceIdType.MESH
NRHS = 16
RANK = 64
LEAVES = 64
POINTS = 4096
SPAN = 256
CHUNKS = POINTS // SPAN
COARSE = POINTS // SPAN

UP_SLOT = {4: 0, 3: 16, 2: 24, 7: 28, 6: 32, 5: 34}
UP_COUNT = {4: 16, 3: 8, 2: 4, 7: 4, 6: 2, 5: 1}

NEAR_PEERS = (4, 5, 6, 7, 2, 3, 1)
Z_HOPS = (0, 1, 2, 3, 4, 3, 2, 3)
Y_HOPS = (0, 1, 2, 1)
FAR_PEERS = tuple(sorted(range(1, 32), key=lambda k: -Z_HOPS[k % 8] - Y_HOPS[k // 8]))


def nn(a, b):
    return lax.dot_general(a, b, (((1,), (0,)), ((), ())), preferred_element_type=F32)


def nt(a, b):
    return lax.dot_general(a, b, (((1,), (1,)), ((), ())), preferred_element_type=F32)


def flipped(index, mask):
    out = index
    for bit in range(8):
        if (mask >> bit) & 1:
            step = 1 << bit
            out = out + step * (1 - 2 * lax.rem(lax.div(index, step), 2))
    return out


def split(x):
    high = x.astype(BF16)
    return high, (x - high.astype(F32)).astype(BF16)


def stacked(x):
    return jnp.concatenate(split(x), axis=0)[:, :RANK]


def folded(x):
    return x[0:NRHS] + x[NRHS : 2 * NRHS]


def swapped(x):
    return pltpu.roll(x, RANK, axis=1)


def kernel(
    offsets_hbm,
    pattern_hbm,
    measured_hbm,
    perm_hbm,
    near_hbm,
    bases_hbm,
    transfer_hbm,
    coupling_hbm,
    root_hbm,
    top_hbm,
    out,
    offsets,
    pattern,
    measured,
    perm,
    near_blocks,
    bases,
    transfer,
    coupling,
    root_row,
    tops,
    climbs,
    group_up,
    reach,
    root_wide,
    perm_rows,
    mix,
    mixed_order,
    mixed_points,
    basis,
    basis_pairs,
    onehot,
    points,
    coef,
    local_terms,
    near_part,
    fields,
    combined,
    edges,
    halo,
    first,
    first_coef,
    second,
    second_coef,
    in_sem,
    top_sem,
    send_sem,
    recv_sem,
    ready,
):
    me = lax.axis_index("leaf")
    right = lax.rem(me + 1, 256)
    left = lax.rem(me + 255, 256)
    low = lax.broadcasted_iota(jnp.int32, (NRHS, 128), 1) < RANK

    loads = [
        pltpu.make_async_copy(source, target, in_sem.at[i])
        for i, (source, target) in enumerate(
            [
                (perm_hbm, perm),
                (measured_hbm, measured),
                (bases_hbm, bases),
                (root_hbm, root_row),
                (transfer_hbm, transfer),
                (coupling_hbm, coupling),
                (near_hbm, near_blocks),
                (pattern_hbm, pattern),
                (offsets_hbm, offsets),
            ]
        )
    ]
    for load in loads[:4]:
        load.start()

    barrier = pltpu.get_barrier_semaphore()
    core = lax.rem(me, 2)
    place = lax.rem(me, 8)

    def tell(device):
        pl.semaphore_signal(barrier, inc=1, device_id=(device,), device_id_type=MESH)

    for k in FAR_PEERS:
        tell(flipped(me - core + 1, 8 * k))

    @pl.when(place == 7)
    def _():
        tell(right)

    @pl.when(place == 0)
    def _():
        tell(left)

    for k in (4, 2, 6):
        tell(flipped(me - core, k))

    @pl.when(core == 1)
    def _():
        tell(me - 1)

    loads[4].start()
    group = lax.div(me, 8)
    top_loads = [
        pltpu.make_async_copy(top_hbm.at[pl.ds(start, count)], tops.at[pl.ds(at, count)], top_sem.at[0])
        for start, at, count in (
            (0, 0, 32),
            (32 + group, 32, 1),
            (64 + 2 * group, 33, 2),
            (128 + 4 * group, 35, 4),
        )
    ]
    for load in top_loads:
        load.start()
    for load in loads[5:]:
        load.start()

    natural = lax.broadcasted_iota(jnp.int32, (SPAN, SPAN), 0)
    column = lax.broadcasted_iota(jnp.int32, (SPAN, SPAN), 1)
    within = lax.rem(column, RANK)
    wanted = column - within + 2 * lax.rem(within, 32) + lax.div(within, 32)
    mix[...] = jnp.where(natural == wanted, 1.0, 0.0).astype(BF16)
    loads[0].wait()
    for c in range(CHUNKS):
        perm_rows[c : c + 1, :] = perm[0:1, c * SPAN : (c + 1) * SPAN]
    order = perm_rows[...]
    digits = jnp.concatenate([lax.rem(order, SPAN), lax.div(order, SPAN)], axis=0)
    mixed = nn(digits.astype(F32).astype(BF16), mix[...])
    mixed_order[...] = mixed.astype(jnp.int32)
    fine_order = mixed.astype(BF16)
    numbers = natural.astype(F32).astype(BF16)
    one, zero = jnp.ones((SPAN, SPAN), BF16), jnp.zeros((SPAN, SPAN), BF16)

    loads[1].wait()
    spread = jnp.concatenate(
        [measured[:, h * SPAN : (h + 1) * SPAN] for h in range(COARSE)], axis=0
    )
    for c in range(CHUNKS):
        at = slice(c * SPAN, (c + 1) * SPAN)
        hot = jnp.where(numbers == fine_order[c : c + 1, :], one, zero)
        onehot[:, at] = hot
        picked = nn(spread, hot)
        coarse = jnp.broadcast_to(mixed_order[COARSE + c : COARSE + c + 1, :], (NRHS, SPAN))
        chosen = picked[0:NRHS]
        for h in range(1, COARSE):
            chosen = jnp.where(coarse == h, picked[h * NRHS : (h + 1) * NRHS], chosen)
        mixed_points[:, at] = chosen.astype(BF16)

    loads[2].wait()
    turn = jnp.where(lax.rem(natural, 8) * 32 + lax.div(natural, 8) == column, 1.0, 0.0).astype(BF16)
    low_half = lax.broadcasted_iota(jnp.int32, (32, 128), 1) < RANK
    for side in range(2):
        rows = slice(side * 32, (side + 1) * 32)
        blocks = []
        for eight in range(4):
            taken = [bases[rows, (8 * eight + k) * 128 : (8 * eight + k + 1) * 128] for k in range(8)]
            blocks.append(nn(turn, jnp.concatenate(taken, axis=0)))
        for leaf in range(32):
            both = jnp.concatenate([block[leaf * 8 : (leaf + 1) * 8] for block in blocks], axis=0)
            turned = swapped(both)
            at = (side * 32 + leaf) * RANK
            basis[at : at + RANK, :] = jnp.concatenate(
                [jnp.where(low_half, both, turned), jnp.where(low_half, turned, both)], axis=0
            ).astype(BF16)

    loads[3].wait()
    low_row = lax.broadcasted_iota(jnp.int32, (1, 128), 1) < RANK
    for pair in range(32):
        both = root_row[0:1, pair * 128 : (pair + 1) * 128].astype(F32)
        turned = swapped(both)
        root_wide[2 * pair : 2 * pair + 1, :] = jnp.where(low_row, both, turned)
        root_wide[2 * pair + 1 : 2 * pair + 2, :] = jnp.where(low_row, turned, both)
    root_map = root_wide[...].astype(BF16)

    quarter = lax.broadcasted_iota(jnp.int32, (NRHS, 256), 1) // RANK
    for four in range(LEAVES // 4):
        chunk = mixed_points[:, four * SPAN : (four + 1) * SPAN].astype(F32)
        block = jnp.concatenate(
            [jnp.where(quarter == k, chunk, 0.0) for k in range(4)], axis=0
        ).astype(BF16)
        result = nn(block, basis[four * 256 : (four + 1) * 256, :])
        for k in range(4):
            coef[64 + 4 * four + k] = jnp.concatenate(
                split(result[k * NRHS : (k + 1) * NRHS]), axis=0
            )

    loads[4].wait()

    def climb(parent):
        children = coef[pl.ds(2 * parent, 2)].reshape(64, 128)[:, :RANK]
        result = nn(children, transfer[parent - 1])
        mixed = jnp.where(low, folded(result[0:32]), folded(result[32:64]))
        return mixed + swapped(mixed)

    for level in range(5, 0, -1):
        groups = 1 << level
        for parent in range(groups, 2 * groups):
            coef[parent] = jnp.concatenate(split(climb(parent)), axis=0)
    root_coef = climb(1)
    root_up = folded(nn(stacked(root_coef), root_map))

    def packed(x):
        high = x.astype(BF16).astype(F32)
        return jnp.where(low, high, x - high).astype(BF16)

    def opened(x):
        return x + swapped(x)

    def send(buffer, slot, mask, at):
        copy = pltpu.make_async_remote_copy(
            src_ref=buffer.at[0],
            dst_ref=buffer.at[slot],
            send_sem=send_sem.at[at],
            recv_sem=recv_sem.at[at],
            device_id=(flipped(me, mask),),
            device_id_type=MESH,
        )
        copy.start()

    def arrived(buffer, at):
        slots = buffer.at[pl.ds(1, buffer.shape[0] - 1)]
        pltpu.make_async_remote_copy(
            src_ref=slots,
            dst_ref=slots,
            send_sem=send_sem.at[at],
            recv_sem=recv_sem.at[at],
            device_id=(flipped(me, 1),),
            device_id_type=MESH,
        ).wait()

    first[0] = packed(root_up)
    first_coef[0] = packed(root_coef)

    def tell_other_core(at):
        pl.semaphore_signal(ready.at[at], inc=1, device_id=(flipped(me, 1),), device_id_type=MESH)

    @pl.when(core == 0)
    def _():
        pl.semaphore_wait(barrier, 7 + lax.div(7 - place, 7))
        tell_other_core(0)

    @pl.when(core == 1)
    def _():
        pl.semaphore_wait(ready.at[0], 1)

    for k in NEAR_PEERS:
        send(first, k, k, 0)
    send(first_coef, 1, 1, 1)
    @pl.when(core == 1)
    def _():
        pl.semaphore_wait(barrier, 62 + lax.div(place, 7))
        tell_other_core(1)

    pltpu.make_async_copy(top_hbm.at[pl.ds(0, 39)], tops, top_sem.at[0]).wait()

    def top_row(level, k):
        if level == 0:
            return 1
        own = lax.div(me, 1 << (8 - level))
        if level < 5:
            return (1 << level) + flipped(own, k)
        if level == 5:
            return 32
        return (33 if level == 6 else 35) + flipped(lax.rem(own, 1 << (level - 5)), k)

    low_rank = lax.broadcasted_iota(jnp.int32, (RANK, 128), 1) < RANK
    for level, count in UP_COUNT.items():
        for k in range(count):
            block = tops[top_row(level, k)].astype(F32)
            climbs[UP_SLOT[level] + k] = jnp.where(low_rank, swapped(block), block).astype(BF16)

    unmixed = nt(
        jnp.concatenate(
            [mixed_points[:, c * SPAN : (c + 1) * SPAN] for c in range(CHUNKS)], axis=0
        ),
        mix[...],
    )
    for m in range(LEAVES // 2):
        c, pair = m // 2, m % 2
        both = unmixed[c * NRHS : (c + 1) * NRHS, pair * 128 : (pair + 1) * 128]
        turned = swapped(both)
        points[2 * m + 2] = jnp.where(low, both, turned).astype(BF16)
        points[2 * m + 3] = jnp.where(low, turned, both).astype(BF16)
        if m == 0:
            edges[0] = both.astype(BF16)
        if m == LEAVES // 2 - 1:
            edges[1] = both.astype(BF16)

    halo_copies = [
        pltpu.make_async_remote_copy(
            src_ref=edges.at[side],
            dst_ref=halo.at[side],
            send_sem=send_sem.at[4],
            recv_sem=recv_sem.at[4],
            device_id=(target,),
            device_id_type=MESH,
        )
        for side, target in ((0, left), (1, right))
    ]
    for copy in halo_copies:
        copy.start()


    def couple(pair):
        sides = []
        for k in range(2):
            n = 2 * pair + k
            sides.append(
                jnp.concatenate(
                    [coef[pattern[0, n]][:, :RANK], coef[pattern[1, n]][:, RANK:]], axis=1
                )
            )
        blocks = coupling[pl.ds(2 * pair, 2)].reshape(128, 128)
        result = nt(jnp.concatenate(sides, axis=0), blocks)
        local_terms[pair + 1] = jnp.where(low, folded(result[0:32]), folded(result[32:64]))

    def near(pair):
        sides = []
        for k in range(2):
            leaf = 2 * pair + k
            at = [points[leaf + 2 + offsets[j, leaf]] for j in range(4)]
            sides.append(
                jnp.concatenate(
                    [at[0][:, :RANK], at[1][:, RANK:], at[2][:, :RANK], at[3][:, RANK:]], axis=1
                )
            )
        blocks = near_blocks[pl.ds(2 * pair, 2)].reshape(128, 256)
        result = nt(jnp.concatenate(sides, axis=0), blocks)
        near_part[pair] = jnp.where(low, result[0:NRHS], result[NRHS : 2 * NRHS])

    def lift(values, level):
        out = []
        for k in range(0, len(values), 2):
            both = jnp.where(low, values[k], values[k + 1])
            blocks = climbs[pl.ds(UP_SLOT[level] + k, 2)].reshape(128, 128)
            out.append(folded(nn(jnp.concatenate(split(both), axis=0), blocks)))
        return out

    def coupled(sibling, level):
        block = tops[top_row(level - 1, 0)]
        parts = stacked(sibling)
        to_left = folded(nt(parts, block[:, :RANK]))
        to_right = folded(nn(parts, block))[:, :RANK]
        odd = lax.rem(lax.div(me, 1 << (8 - level)), 2)
        return jnp.where(odd == 1, to_right, to_left)

    def received(buffer, k):
        return opened(buffer[k].astype(F32) + buffer[k + 1].astype(F32))

    def pairs_of(values):
        wide = [jnp.where(low, values[k], values[k + 1]) for k in range(0, len(values), 2)]
        return jnp.concatenate(split(jnp.concatenate(wide, axis=1)), axis=0)

    for side in range(2):
        inner = split(nn(climbs[UP_SLOT[6] + side][:, :RANK], climbs[UP_SLOT[5]]))
        for k in (2 * side, 2 * side + 1):
            outer = climbs[UP_SLOT[7] + k][:, :RANK]
            high, rest = split(nn(outer, inner[0]) + nn(outer, inner[1]))
            group_up[k * RANK : (k + 1) * RANK, :] = jnp.where(
                low_rank, high.astype(F32), rest.astype(F32)
            ).astype(BF16)

    terms = {}
    arrived(first, 0)
    at_7 = [received(first, 2 * k) for k in range(4)]
    second[0] = packed(opened(folded(nn(pairs_of(at_7), group_up[...]))))

    @pl.when(core == 0)
    def _():
        pl.semaphore_wait(ready.at[1], 1)

    for k in FAR_PEERS:
        send(second, k, 8 * k, 2)
    at_6 = lift(at_7, 7)
    at_5 = lift(at_6, 6)[0]
    second_coef[0] = packed(at_5)
    send(second_coef, 1, 8, 3)
    def stacked_rows(x):
        return jnp.concatenate(split(x), axis=0)

    def folded_rows(x):
        return x[0:RANK] + x[RANK : 2 * RANK]

    def times(x, block):
        return folded_rows(nn(stacked_rows(x), block))

    def times_turned(x, blocks):
        return folded_rows(nt(stacked_rows(x), blocks))

    def outward(x, level, k):
        blocks = climbs[pl.ds(UP_SLOT[level] + k, 2)].reshape(128, 128)[:, :RANK]
        return times_turned(x, blocks)

    def halves(x):
        return [x[:, :RANK], swapped(x)[:, :RANK]]

    down = {7: root_map[:, :RANK].astype(F32)}
    for level in range(6, 0, -1):
        down[level] = times(down[level + 1], climbs[UP_SLOT[level + 1]])[:, :RANK]

    def crossing(level):
        block = tops[top_row(level - 1, 0)]
        to_left = times(down[level], block)[:, :RANK]
        to_right = times_turned(down[level], block[:, :RANK])
        odd = lax.rem(lax.div(me, 1 << (8 - level)), 2)
        return jnp.where(odd == 1, to_right, to_left)

    by_pair = [jnp.concatenate([jnp.zeros((RANK, RANK), F32), crossing(4)], axis=1)]
    by_pair.append(outward(crossing(3), 4, 2))
    for j, part in enumerate(halves(outward(crossing(2), 3, 2))):
        by_pair.append(outward(part, 4, 4 + 2 * j))
    for i, outer in enumerate(halves(outward(crossing(1), 2, 2))):
        for j, part in enumerate(halves(outward(outer, 3, 4 + 2 * i))):
            by_pair.append(outward(part, 4, 8 + 4 * i + 2 * j))
    for p in range(8):
        reach[:, p * 128 : (p + 1) * 128] = stacked_rows(by_pair[p])

    arrived(first_coef, 1)
    terms[8] = coupled(opened(first_coef[1].astype(F32)), 8)
    terms[7] = coupled(at_7[1], 7)
    terms[6] = coupled(at_6[1], 6)

    for m in range(32):
        basis_pairs[m] = jnp.where(
            low_rank,
            basis[m * 128 : m * 128 + RANK, :].astype(F32),
            basis[m * 128 + RANK : (m + 1) * 128, :].astype(F32),
        ).astype(BF16)

    loads[5].wait()
    loads[7].wait()

    @pl.loop(0, 9)
    def _(step):
        for k in range(7):
            couple(7 * step + k)

    pltpu.make_async_remote_copy(
        src_ref=edges,
        dst_ref=halo,
        send_sem=send_sem.at[4],
        recv_sem=recv_sem.at[4],
        device_id=(left,),
        device_id_type=MESH,
    ).wait()
    for side, leaf, end in ((1, 0, 0), (0, 66, 255)):
        both = jnp.where(me == end, 0.0, halo[side].astype(F32))
        turned = swapped(both)
        points[leaf] = jnp.where(low, both, turned).astype(BF16)
        points[leaf + 1] = jnp.where(low, turned, both).astype(BF16)
    loads[6].wait()
    loads[8].wait()

    @pl.loop(0, 4)
    def _(step):
        for k in range(8):
            near(8 * step + k)

    naturals = jnp.concatenate([near_part[m] for m in range(LEAVES // 2)], axis=0)
    high, rest = split(naturals)
    mixer = mix[0:128, 0:128]
    turned = nn(high, mixer) + nn(rest, mixer)
    for m in range(LEAVES // 2):
        near_part[m] = turned[m * NRHS : (m + 1) * NRHS]

    arrived(second_coef, 3)
    field = coupled(opened(second_coef[1].astype(F32)), 5)
    for level in (6, 7):
        block = climbs[UP_SLOT[level]][:, :RANK]
        field = terms[level] + folded(nt(stacked(field), block))
    field = terms[8] + folded(nt(stacked(field), root_map[:, :RANK]))
    near_field = jnp.concatenate([field, field], axis=1)

    arrived(second, 2)
    at_4 = [received(second, 2 * k) for k in range(16)]
    root_field = near_field + opened(folded(nt(pairs_of(at_4), reach[...])))

    def descend(parent, here, there):
        lhs = jnp.concatenate(
            [jnp.where(low, part, 0.0) for part in here]
            + [jnp.where(low, 0.0, part) for part in there],
            axis=0,
        ).astype(BF16)
        result = nt(lhs, transfer[parent - 1])
        fields[parent] = local_terms[parent] + side_by_side(result)

    def side_by_side(result):
        return jnp.concatenate([folded(result[0:32]), folded(result[32:64])], axis=1)

    def parts_of(x):
        high = x.astype(BF16).astype(F32)
        return high, x - high

    root_parts = parts_of(root_field)
    descend(1, root_parts, root_parts)
    for level in range(5):
        for q in range(1 << level, 2 << level):
            pair = fields[q]
            straight = parts_of(pair)
            crossed = parts_of(swapped(pair))
            descend(2 * q, straight, crossed)
            descend(2 * q + 1, crossed, straight)

    for m in range(32):
        pair = fields[32 + m]
        high, rest = parts_of(pair)
        lhs = jnp.concatenate(
            [jnp.where(low, high, 0.0), jnp.where(low, rest, 0.0)]
            + [jnp.where(low, 0.0, high), jnp.where(low, 0.0, rest)],
            axis=0,
        ).astype(BF16)
        whole = near_part[m] + side_by_side(nt(lhs, basis_pairs[m]))
        combined[:, m * 128 : (m + 1) * 128] = jnp.concatenate(parts_of(whole), axis=0)

    total = jnp.zeros((COARSE * 32, SPAN), F32)
    for c in range(CHUNKS):
        at = slice(c * SPAN, (c + 1) * SPAN)
        coarse = jnp.broadcast_to(mixed_order[COARSE + c : COARSE + c + 1, :], (32, SPAN))
        values = combined[:, at]
        lhs = jnp.concatenate(
            [jnp.where(coarse == h, values, 0.0) for h in range(COARSE)], axis=0
        ).astype(BF16)
        total = total + nt(lhs, onehot[:, at])
    for h in range(COARSE):
        out[:, h * SPAN : (h + 1) * SPAN] = folded(total[h * 32 : (h + 1) * 32])


def body(
    measured,
    cluster_perm,
    near_offsets,
    near_blocks,
    leaf_bases,
    local_transfer,
    coupling_pattern,
    local_coupling,
    root_transfer,
    top_blocks,
):
    hbm = pl.BlockSpec(memory_space=pl.ANY)
    dma = pltpu.SemaphoreType.DMA
    return pl.pallas_call(
        kernel,
        out_shape=jax.ShapeDtypeStruct((NRHS, POINTS), F32),
        in_specs=[hbm] * 10,
        out_specs=pl.BlockSpec(memory_space=pltpu.VMEM),
        scratch_shapes=[
            pltpu.SMEM((4, 64), jnp.int32),
            pltpu.SMEM((2, 126), jnp.int32),
            pltpu.VMEM((NRHS, POINTS), BF16),
            pltpu.VMEM((1, POINTS), jnp.int32),
            pltpu.VMEM((64, 64, 256), BF16),
            pltpu.VMEM((64, 4096), BF16),
            pltpu.VMEM((63, 64, 128), BF16),
            pltpu.VMEM((126, 64, 128), BF16),
            pltpu.VMEM((1, 4096), BF16),
            pltpu.VMEM((39, 64, 128), BF16),
            pltpu.VMEM((35, 64, 128), BF16),
            pltpu.VMEM((256, 128), BF16),
            pltpu.VMEM((128, 1024), BF16),
            pltpu.VMEM((64, 128), F32),
            pltpu.VMEM((CHUNKS, SPAN), jnp.int32),
            pltpu.VMEM((SPAN, SPAN), BF16),
            pltpu.VMEM((2 * CHUNKS, SPAN), jnp.int32),
            pltpu.VMEM((NRHS, POINTS), BF16),
            pltpu.VMEM((4096, 128), BF16),
            pltpu.VMEM((32, 64, 128), BF16),
            pltpu.VMEM((SPAN, POINTS), BF16),
            pltpu.VMEM((68, NRHS, 128), BF16),
            pltpu.VMEM((128, 2 * NRHS, 128), BF16),
            pltpu.VMEM((64, NRHS, 128), F32),
            pltpu.VMEM((32, NRHS, 128), F32),
            pltpu.VMEM((64, NRHS, 128), F32),
            pltpu.VMEM((2 * NRHS, POINTS), F32),
            pltpu.VMEM((2, NRHS, 128), BF16),
            pltpu.VMEM((2, NRHS, 128), BF16),
            pltpu.VMEM((8, NRHS, 128), BF16),
            pltpu.VMEM((2, NRHS, 128), BF16),
            pltpu.VMEM((32, NRHS, 128), BF16),
            pltpu.VMEM((2, NRHS, 128), BF16),
            dma((9,)),
            dma((1,)),
            dma((5,)),
            dma((5,)),
            pltpu.SemaphoreType.REGULAR((2,)),
        ],
        compiler_params=pltpu.CompilerParams(
            collective_id=0, has_side_effects=True, vmem_limit_bytes=62 * 1024 * 1024
        ),
    )(
        near_offsets.T,
        coupling_pattern.T,
        measured,
        cluster_perm,
        near_blocks,
        leaf_bases,
        local_transfer,
        local_coupling,
        root_transfer,
        top_blocks,
    )


def solution(mesh):
    return jax.shard_map(
        body,
        mesh=mesh,
        in_specs=(
            P(None, "leaf"),
            P("leaf", None),
            P("leaf", None),
            P("leaf", None, None),
            P("leaf", None),
            P("leaf", None, None),
            P("leaf", None),
            P("leaf", None, None),
            P("leaf", None),
            P(),
        ),
        out_specs=P(None, "leaf"),
        check_vma=False,
    )
```

```python
import jax
import jax.numpy as jnp
from jax import lax
from jax.experimental import pallas as pl
from jax.experimental.pallas import tpu as pltpu
from jax.sharding import PartitionSpec as P

F32 = jnp.float32
BF16 = jnp.bfloat16
MESH = pl.DeviceIdType.MESH
NRHS = 16
RANK = 64
LEAVES = 64
POINTS = 4096
SPAN = 256
CHUNKS = POINTS // SPAN
COARSE = POINTS // SPAN

UP_SLOT = {4: 0, 3: 16, 2: 24, 7: 28, 6: 32, 5: 34}
UP_COUNT = {4: 16, 3: 8, 2: 4, 7: 4, 6: 2, 5: 1}

NEAR_PEERS = (4, 5, 6, 7, 2, 3, 1)
Z_HOPS = (0, 1, 2, 3, 4, 3, 2, 3)
Y_HOPS = (0, 1, 2, 1)
FAR_PEERS = tuple(sorted(range(1, 32), key=lambda k: -Z_HOPS[k % 8] - Y_HOPS[k // 8]))


def nn(a, b):
    return lax.dot_general(a, b, (((1,), (0,)), ((), ())), preferred_element_type=F32)


def nt(a, b):
    return lax.dot_general(a, b, (((1,), (1,)), ((), ())), preferred_element_type=F32)


def flipped(index, mask):
    out = index
    for bit in range(8):
        if (mask >> bit) & 1:
            step = 1 << bit
            out = out + step * (1 - 2 * lax.rem(lax.div(index, step), 2))
    return out


def split(x):
    high = x.astype(BF16)
    return high, (x - high.astype(F32)).astype(BF16)


def stacked(x):
    return jnp.concatenate(split(x), axis=0)[:, :RANK]


def folded(x):
    return x[0:NRHS] + x[NRHS : 2 * NRHS]


def swapped(x):
    return pltpu.roll(x, RANK, axis=1)


def kernel(
    offsets_hbm,
    pattern_hbm,
    measured_hbm,
    perm_hbm,
    near_hbm,
    bases_hbm,
    transfer_hbm,
    coupling_hbm,
    root_hbm,
    top_hbm,
    out,
    offsets,
    pattern,
    measured,
    perm,
    near_blocks,
    bases,
    transfer,
    coupling,
    root_row,
    tops,
    climbs,
    group_up,
    local_map,
    up_map,
    reach,
    root_rows,
    root_wide,
    perm_rows,
    mix,
    mixed_order,
    mixed_points,
    basis,
    basis_pairs,
    onehot,
    points,
    coef,
    local_terms,
    near_part,
    fields,
    combined,
    edges,
    halo,
    first,
    first_coef,
    second,
    second_coef,
    in_sem,
    top_sem,
    send_sem,
    recv_sem,
    ready,
):
    me = lax.axis_index("leaf")
    right = lax.rem(me + 1, 256)
    left = lax.rem(me + 255, 256)
    low = lax.broadcasted_iota(jnp.int32, (NRHS, 128), 1) < RANK

    loads = [
        pltpu.make_async_copy(source, target, in_sem.at[i])
        for i, (source, target) in enumerate(
            [
                (perm_hbm, perm),
                (measured_hbm, measured),
                (bases_hbm, bases),
                (root_hbm, root_row),
                (transfer_hbm, transfer),
                (coupling_hbm, coupling),
                (near_hbm, near_blocks),
                (pattern_hbm, pattern),
                (offsets_hbm, offsets),
            ]
        )
    ]
    for load in loads[:4]:
        load.start()

    barrier = pltpu.get_barrier_semaphore()
    core = lax.rem(me, 2)
    place = lax.rem(me, 8)

    def tell(device):
        pl.semaphore_signal(barrier, inc=1, device_id=(device,), device_id_type=MESH)

    @pl.when(place == 7)
    def _():
        tell(right)

    @pl.when(place == 0)
    def _():
        tell(left)

    for k in (4, 2, 6):
        tell(flipped(me - core, k))

    @pl.when(core == 1)
    def _():
        tell(me - 1)

    for k in FAR_PEERS:
        tell(flipped(me - core + 1, 8 * k))

    loads[4].start()
    natural = lax.broadcasted_iota(jnp.int32, (SPAN, SPAN), 0)
    column = lax.broadcasted_iota(jnp.int32, (SPAN, SPAN), 1)
    within = lax.rem(column, RANK)
    wanted = column - within + 2 * lax.rem(within, 32) + lax.div(within, 32)
    mix[...] = jnp.where(natural == wanted, 1.0, 0.0).astype(BF16)
    loads[0].wait()
    for c in range(CHUNKS):
        perm_rows[c : c + 1, :] = perm[0:1, c * SPAN : (c + 1) * SPAN]
    order = perm_rows[...]
    digits = jnp.concatenate([lax.rem(order, SPAN), lax.div(order, SPAN)], axis=0)
    mixed = nn(digits.astype(F32).astype(BF16), mix[...])
    mixed_order[...] = mixed.astype(jnp.int32)
    fine_order = mixed.astype(BF16)
    numbers = natural.astype(F32).astype(BF16)
    one, zero = jnp.ones((SPAN, SPAN), BF16), jnp.zeros((SPAN, SPAN), BF16)

    loads[1].wait()
    loads[2].wait()
    loads[3].wait()
    group = lax.div(me, 8)
    top_loads = [
        pltpu.make_async_copy(top_hbm.at[pl.ds(start, count)], tops.at[pl.ds(at, count)], top_sem.at[0])
        for start, at, count in (
            (0, 0, 32),
            (32 + group, 32, 1),
            (64 + 2 * group, 33, 2),
            (128 + 4 * group, 35, 4),
        )
    ]
    for load in top_loads:
        load.start()
    for load in loads[5:]:
        load.start()
    for pair in range(32):
        root_rows[pair : pair + 1, :] = root_row[0:1, pair * 128 : (pair + 1) * 128].astype(F32)
    both = root_rows[...]
    turned = swapped(both)
    low_half = lax.broadcasted_iota(jnp.int32, (32, 128), 1) < RANK
    root_wide[pl.ds(0, 32, stride=2), :] = jnp.where(low_half, both, turned)
    root_wide[pl.ds(1, 32, stride=2), :] = jnp.where(low_half, turned, both)
    root_map = root_wide[...].astype(BF16)

    spread = jnp.concatenate(
        [measured[:, h * SPAN : (h + 1) * SPAN] for h in range(COARSE)], axis=0
    )
    for c in range(CHUNKS):
        at = slice(c * SPAN, (c + 1) * SPAN)
        hot = jnp.where(numbers == fine_order[c : c + 1, :], one, zero)
        onehot[:, at] = hot
        picked = nn(spread, hot)
        coarse = jnp.broadcast_to(mixed_order[COARSE + c : COARSE + c + 1, :], (NRHS, SPAN))
        chosen = picked[0:NRHS]
        for h in range(1, COARSE):
            chosen = jnp.where(coarse == h, picked[h * NRHS : (h + 1) * NRHS], chosen)
        mixed_points[:, at] = chosen.astype(BF16)

    loads[4].wait()
    low_rank = lax.broadcasted_iota(jnp.int32, (RANK, 128), 1) < RANK

    def opened(x):
        return x + swapped(x)

    def both_parts(x):
        high = x.astype(BF16).astype(F32)
        return jnp.where(low_rank, high, x - high).astype(BF16)

    def folded_rows(x):
        return x[0:RANK] + x[RANK : 2 * RANK]

    first_pair = transfer[0].astype(F32)
    maps = {
        2: jnp.where(low_rank, first_pair, 0.0).astype(BF16),
        3: jnp.where(low_rank, swapped(first_pair), 0.0).astype(BF16),
    }
    products = {}

    def multiply(slot):
        block = transfer[slot // 2 - 1]
        step = block[:, :RANK] if slot % 2 == 0 else block[:, RANK:]
        products[slot] = opened(nn(step, maps[slot // 2]))
        maps[slot] = both_parts(products[slot])
        if slot >= 8:
            local_map[slot - 8] = maps[slot]

    def through_root(slot):
        rows = jnp.concatenate(split(products[slot]), axis=0)[:, :RANK]
        up_map[slot - 8] = both_parts(folded_rows(nn(rows, root_map)))

    tasks = [(multiply, slot) for slot in range(4, 16)] + [(through_root, slot) for slot in range(8, 16)]

    turn = jnp.where(lax.rem(natural, 8) * 32 + lax.div(natural, 8) == column, 1.0, 0.0).astype(BF16)
    low_half = lax.broadcasted_iota(jnp.int32, (32, 128), 1) < RANK
    for side in range(2):
        rows = slice(side * 32, (side + 1) * 32)
        blocks = []
        for eight in range(4):
            taken = [bases[rows, (8 * eight + k) * 128 : (8 * eight + k + 1) * 128] for k in range(8)]
            blocks.append(nn(turn, jnp.concatenate(taken, axis=0)))
        for leaf in range(32):
            both = jnp.concatenate([block[leaf * 8 : (leaf + 1) * 8] for block in blocks], axis=0)
            turned = swapped(both)
            at = (side * 32 + leaf) * RANK
            basis[at : at + RANK, :] = jnp.concatenate(
                [jnp.where(low_half, both, turned), jnp.where(low_half, turned, both)], axis=0
            ).astype(BF16)
            if leaf % 3 == 0 and tasks:
                task, slot = tasks.pop(0)
                task(slot)

    quarter = lax.broadcasted_iota(jnp.int32, (NRHS, 256), 1) // RANK
    for four in range(LEAVES // 4):
        chunk = mixed_points[:, four * SPAN : (four + 1) * SPAN].astype(F32)
        block = jnp.concatenate(
            [jnp.where(quarter == k, chunk, 0.0) for k in range(4)], axis=0
        ).astype(BF16)
        result = nn(block, basis[four * 256 : (four + 1) * 256, :])
        for k in range(4):
            coef[64 + 4 * four + k] = jnp.concatenate(
                split(result[k * NRHS : (k + 1) * NRHS]), axis=0
            )

    def climb(parent):
        children = coef[pl.ds(2 * parent, 2)].reshape(64, 128)[:, :RANK]
        result = nn(children, transfer[parent - 1])
        mixed = jnp.where(low, folded(result[0:32]), folded(result[32:64]))
        return mixed + swapped(mixed)

    def climb_levels(levels):
        for level in levels:
            values = []
            for parent in range(1 << level, 2 << level):
                values.append(climb(parent))
                coef[parent] = jnp.concatenate(split(values[-1]), axis=0)
        return values

    def pairs_of(values):
        wide = [jnp.where(low, values[k], values[k + 1]) for k in range(0, len(values), 2)]
        return jnp.concatenate(split(jnp.concatenate(wide, axis=1)), axis=0)

    depth_3 = climb_levels((5, 4, 3))
    root_up = opened(folded(nn(pairs_of(depth_3), up_map[...].reshape(512, 128))))

    def packed(x):
        high = x.astype(BF16).astype(F32)
        return jnp.where(low, high, x - high).astype(BF16)

    def send(buffer, slot, mask, at):
        copy = pltpu.make_async_remote_copy(
            src_ref=buffer.at[0],
            dst_ref=buffer.at[slot],
            send_sem=send_sem.at[at],
            recv_sem=recv_sem.at[at],
            device_id=(flipped(me, mask),),
            device_id_type=MESH,
        )
        copy.start()

    def arrived(buffer, at):
        slots = buffer.at[pl.ds(1, buffer.shape[0] - 1)]
        pltpu.make_async_remote_copy(
            src_ref=slots,
            dst_ref=slots,
            send_sem=send_sem.at[at],
            recv_sem=recv_sem.at[at],
            device_id=(flipped(me, 1),),
            device_id_type=MESH,
        ).wait()

    first[0] = packed(root_up)

    def tell_other_core(at):
        pl.semaphore_signal(ready.at[at], inc=1, device_id=(flipped(me, 1),), device_id_type=MESH)

    @pl.when(core == 0)
    def _():
        pl.semaphore_wait(barrier, 7 + lax.div(7 - place, 7))
        tell_other_core(0)

    @pl.when(core == 1)
    def _():
        pl.semaphore_wait(ready.at[0], 1)

    for k in NEAR_PEERS:
        send(first, k, k, 0)
    @pl.when(core == 1)
    def _():
        pl.semaphore_wait(barrier, 62 + lax.div(place, 7))
        tell_other_core(1)

    climb_levels((2, 1))
    first_coef[0] = packed(climb(1))
    send(first_coef, 1, 1, 1)

    pltpu.make_async_copy(top_hbm.at[pl.ds(0, 39)], tops, top_sem.at[0]).wait()

    def top_row(level, k):
        if level == 0:
            return 1
        own = lax.div(me, 1 << (8 - level))
        if level < 5:
            return (1 << level) + flipped(own, k)
        if level == 5:
            return 32
        return (33 if level == 6 else 35) + flipped(lax.rem(own, 1 << (level - 5)), k)

    for level, count in UP_COUNT.items():
        for k in range(count):
            block = tops[top_row(level, k)].astype(F32)
            climbs[UP_SLOT[level] + k] = jnp.where(low_rank, swapped(block), block).astype(BF16)

    unmixed = nt(
        jnp.concatenate(
            [mixed_points[:, c * SPAN : (c + 1) * SPAN] for c in range(CHUNKS)], axis=0
        ),
        mix[...],
    )
    for m in range(LEAVES // 2):
        c, pair = m // 2, m % 2
        both = unmixed[c * NRHS : (c + 1) * NRHS, pair * 128 : (pair + 1) * 128]
        turned = swapped(both)
        points[2 * m + 2] = jnp.where(low, both, turned).astype(BF16)
        points[2 * m + 3] = jnp.where(low, turned, both).astype(BF16)
        if m == 0:
            edges[0] = both.astype(BF16)
        if m == LEAVES // 2 - 1:
            edges[1] = both.astype(BF16)

    halo_copies = [
        pltpu.make_async_remote_copy(
            src_ref=edges.at[side],
            dst_ref=halo.at[side],
            send_sem=send_sem.at[4],
            recv_sem=recv_sem.at[4],
            device_id=(target,),
            device_id_type=MESH,
        )
        for side, target in ((0, left), (1, right))
    ]
    for copy in halo_copies:
        copy.start()


    def couple(pair):
        sides = []
        for k in range(2):
            n = 2 * pair + k
            sides.append(
                jnp.concatenate(
                    [coef[pattern[0, n]][:, :RANK], coef[pattern[1, n]][:, RANK:]], axis=1
                )
            )
        blocks = coupling[pl.ds(2 * pair, 2)].reshape(128, 128)
        result = nt(jnp.concatenate(sides, axis=0), blocks)
        local_terms[pair + 1] = jnp.where(low, folded(result[0:32]), folded(result[32:64]))

    def near(pair):
        sides = []
        for k in range(2):
            leaf = 2 * pair + k
            at = [points[leaf + 2 + offsets[j, leaf]] for j in range(4)]
            sides.append(
                jnp.concatenate(
                    [at[0][:, :RANK], at[1][:, RANK:], at[2][:, :RANK], at[3][:, RANK:]], axis=1
                )
            )
        blocks = near_blocks[pl.ds(2 * pair, 2)].reshape(128, 256)
        result = nt(jnp.concatenate(sides, axis=0), blocks)
        near_part[pair] = jnp.where(low, result[0:NRHS], result[NRHS : 2 * NRHS])

    def lift(values, level):
        out = []
        for k in range(0, len(values), 2):
            both = jnp.where(low, values[k], values[k + 1])
            blocks = climbs[pl.ds(UP_SLOT[level] + k, 2)].reshape(128, 128)
            out.append(folded(nn(jnp.concatenate(split(both), axis=0), blocks)))
        return out

    def coupled(sibling, level):
        block = tops[top_row(level - 1, 0)]
        parts = stacked(sibling)
        to_left = folded(nt(parts, block[:, :RANK]))
        to_right = folded(nn(parts, block))[:, :RANK]
        odd = lax.rem(lax.div(me, 1 << (8 - level)), 2)
        return jnp.where(odd == 1, to_right, to_left)

    def received(buffer, k):
        return opened(buffer[k].astype(F32) + buffer[k + 1].astype(F32))

    for side in range(2):
        inner = split(nn(climbs[UP_SLOT[6] + side][:, :RANK], climbs[UP_SLOT[5]]))
        for k in (2 * side, 2 * side + 1):
            outer = climbs[UP_SLOT[7] + k][:, :RANK]
            high, rest = split(nn(outer, inner[0]) + nn(outer, inner[1]))
            group_up[k * RANK : (k + 1) * RANK, :] = jnp.where(
                low_rank, high.astype(F32), rest.astype(F32)
            ).astype(BF16)

    terms = {}
    arrived(first, 0)
    at_7 = [received(first, 2 * k) for k in range(4)]
    second[0] = packed(opened(folded(nn(pairs_of(at_7), group_up[...]))))

    @pl.when(core == 0)
    def _():
        pl.semaphore_wait(ready.at[1], 1)

    for k in FAR_PEERS:
        send(second, k, 8 * k, 2)
    at_6 = lift(at_7, 7)
    at_5 = lift(at_6, 6)[0]
    second_coef[0] = packed(at_5)
    send(second_coef, 1, 8, 3)
    def stacked_rows(x):
        return jnp.concatenate(split(x), axis=0)

    def times(x, block):
        return folded_rows(nn(stacked_rows(x), block))

    def times_turned(x, blocks):
        return folded_rows(nt(stacked_rows(x), blocks))

    def outward(x, level, k):
        blocks = climbs[pl.ds(UP_SLOT[level] + k, 2)].reshape(128, 128)[:, :RANK]
        return times_turned(x, blocks)

    def halves(x):
        return [x[:, :RANK], swapped(x)[:, :RANK]]

    down = {7: root_map[:, :RANK].astype(F32)}
    for level in range(6, 0, -1):
        down[level] = times(down[level + 1], climbs[UP_SLOT[level + 1]])[:, :RANK]

    def crossing(level):
        block = tops[top_row(level - 1, 0)]
        to_left = times(down[level], block)[:, :RANK]
        to_right = times_turned(down[level], block[:, :RANK])
        odd = lax.rem(lax.div(me, 1 << (8 - level)), 2)
        return jnp.where(odd == 1, to_right, to_left)

    by_pair = [jnp.concatenate([jnp.zeros((RANK, RANK), F32), crossing(4)], axis=1)]
    by_pair.append(outward(crossing(3), 4, 2))
    for j, part in enumerate(halves(outward(crossing(2), 3, 2))):
        by_pair.append(outward(part, 4, 4 + 2 * j))
    for i, outer in enumerate(halves(outward(crossing(1), 2, 2))):
        for j, part in enumerate(halves(outward(outer, 3, 4 + 2 * i))):
            by_pair.append(outward(part, 4, 8 + 4 * i + 2 * j))
    for p in range(8):
        reach[:, p * 128 : (p + 1) * 128] = stacked_rows(by_pair[p])

    arrived(first_coef, 1)
    terms[8] = coupled(opened(first_coef[1].astype(F32)), 8)
    terms[7] = coupled(at_7[1], 7)
    terms[6] = coupled(at_6[1], 6)

    for m in range(32):
        basis_pairs[m] = jnp.where(
            low_rank,
            basis[m * 128 : m * 128 + RANK, :].astype(F32),
            basis[m * 128 + RANK : (m + 1) * 128, :].astype(F32),
        ).astype(BF16)

    loads[5].wait()
    loads[7].wait()

    @pl.loop(0, 9)
    def _(step):
        for k in range(7):
            couple(7 * step + k)

    pltpu.make_async_remote_copy(
        src_ref=edges,
        dst_ref=halo,
        send_sem=send_sem.at[4],
        recv_sem=recv_sem.at[4],
        device_id=(left,),
        device_id_type=MESH,
    ).wait()
    for side, leaf, end in ((1, 0, 0), (0, 66, 255)):
        both = jnp.where(me == end, 0.0, halo[side].astype(F32))
        turned = swapped(both)
        points[leaf] = jnp.where(low, both, turned).astype(BF16)
        points[leaf + 1] = jnp.where(low, turned, both).astype(BF16)
    loads[6].wait()
    loads[8].wait()

    @pl.loop(0, 4)
    def _(step):
        for k in range(8):
            near(8 * step + k)

    arrived(second_coef, 3)
    def descend(parent, here, there):
        lhs = jnp.concatenate(
            [jnp.where(low, part, 0.0) for part in here]
            + [jnp.where(low, 0.0, part) for part in there],
            axis=0,
        ).astype(BF16)
        result = nt(lhs, transfer[parent - 1])
        fields[parent] = local_terms[parent] + side_by_side(result)

    def side_by_side(result):
        return jnp.concatenate([folded(result[0:32]), folded(result[32:64])], axis=1)

    def parts_of(x):
        high = x.astype(BF16).astype(F32)
        return high, x - high

    def descend_levels(levels):
        for level in levels:
            for q in range(1 << level, 2 << level):
                pair = fields[q]
                straight = parts_of(pair)
                crossed = parts_of(swapped(pair))
                descend(2 * q, straight, crossed)
                descend(2 * q + 1, crossed, straight)

    fields[1] = local_terms[1]
    descend_levels((0, 1))

    naturals = jnp.concatenate([near_part[m] for m in range(LEAVES // 2)], axis=0)
    high, rest = split(naturals)
    mixer = mix[0:128, 0:128]
    turned = nn(high, mixer) + nn(rest, mixer)
    for m in range(LEAVES // 2):
        near_part[m] = turned[m * NRHS : (m + 1) * NRHS]

    field = coupled(opened(second_coef[1].astype(F32)), 5)
    for level in (6, 7):
        block = climbs[UP_SLOT[level]][:, :RANK]
        field = terms[level] + folded(nt(stacked(field), block))
    field = terms[8] + folded(nt(stacked(field), root_map[:, :RANK]))
    near_field = jnp.concatenate([field, field], axis=1)

    arrived(second, 2)
    at_4 = [received(second, 2 * k) for k in range(16)]
    root_field = near_field + opened(folded(nt(pairs_of(at_4), reach[...])))

    arriving = folded(
        nt(jnp.concatenate(split(root_field), axis=0), local_map[...].reshape(512, 128))
    )
    for p in range(4, 8):
        fields[p] = fields[p] + arriving[:, (p - 4) * 128 : (p - 3) * 128]
    descend_levels((2, 3, 4))

    for m in range(32):
        pair = fields[32 + m]
        high, rest = parts_of(pair)
        lhs = jnp.concatenate(
            [jnp.where(low, high, 0.0), jnp.where(low, rest, 0.0)]
            + [jnp.where(low, 0.0, high), jnp.where(low, 0.0, rest)],
            axis=0,
        ).astype(BF16)
        whole = near_part[m] + side_by_side(nt(lhs, basis_pairs[m]))
        combined[:, m * 128 : (m + 1) * 128] = jnp.concatenate(parts_of(whole), axis=0)

    total = jnp.zeros((COARSE * 32, SPAN), F32)
    for c in range(CHUNKS):
        at = slice(c * SPAN, (c + 1) * SPAN)
        coarse = jnp.broadcast_to(mixed_order[COARSE + c : COARSE + c + 1, :], (32, SPAN))
        values = combined[:, at]
        lhs = jnp.concatenate(
            [jnp.where(coarse == h, values, 0.0) for h in range(COARSE)], axis=0
        ).astype(BF16)
        total = total + nt(lhs, onehot[:, at])
    for h in range(COARSE):
        out[:, h * SPAN : (h + 1) * SPAN] = folded(total[h * 32 : (h + 1) * 32])


def body(
    measured,
    cluster_perm,
    near_offsets,
    near_blocks,
    leaf_bases,
    local_transfer,
    coupling_pattern,
    local_coupling,
    root_transfer,
    top_blocks,
):
    hbm = pl.BlockSpec(memory_space=pl.ANY)
    dma = pltpu.SemaphoreType.DMA
    return pl.pallas_call(
        kernel,
        out_shape=pltpu.VMEM((NRHS, POINTS), F32),
        in_specs=[hbm] * 10,
        out_specs=pl.BlockSpec(memory_space=pltpu.VMEM),
        scratch_shapes=[
            pltpu.SMEM((4, 64), jnp.int32),
            pltpu.SMEM((2, 126), jnp.int32),
            pltpu.VMEM((NRHS, POINTS), BF16),
            pltpu.VMEM((1, POINTS), jnp.int32),
            pltpu.VMEM((64, 64, 256), BF16),
            pltpu.VMEM((64, 4096), BF16),
            pltpu.VMEM((63, 64, 128), BF16),
            pltpu.VMEM((126, 64, 128), BF16),
            pltpu.VMEM((1, 4096), BF16),
            pltpu.VMEM((39, 64, 128), BF16),
            pltpu.VMEM((35, 64, 128), BF16),
            pltpu.VMEM((256, 128), BF16),
            pltpu.VMEM((8, 64, 128), BF16),
            pltpu.VMEM((8, 64, 128), BF16),
            pltpu.VMEM((128, 1024), BF16),
            pltpu.VMEM((32, 128), F32),
            pltpu.VMEM((64, 128), F32),
            pltpu.VMEM((CHUNKS, SPAN), jnp.int32),
            pltpu.VMEM((SPAN, SPAN), BF16),
            pltpu.VMEM((2 * CHUNKS, SPAN), jnp.int32),
            pltpu.VMEM((NRHS, POINTS), BF16),
            pltpu.VMEM((4096, 128), BF16),
            pltpu.VMEM((32, 64, 128), BF16),
            pltpu.VMEM((SPAN, POINTS), BF16),
            pltpu.VMEM((68, NRHS, 128), BF16),
            pltpu.VMEM((128, 2 * NRHS, 128), BF16),
            pltpu.VMEM((64, NRHS, 128), F32),
            pltpu.VMEM((32, NRHS, 128), F32),
            pltpu.VMEM((64, NRHS, 128), F32),
            pltpu.VMEM((2 * NRHS, POINTS), F32),
            pltpu.VMEM((2, NRHS, 128), BF16),
            pltpu.VMEM((2, NRHS, 128), BF16),
            pltpu.VMEM((8, NRHS, 128), BF16),
            pltpu.VMEM((2, NRHS, 128), BF16),
            pltpu.VMEM((32, NRHS, 128), BF16),
            pltpu.VMEM((2, NRHS, 128), BF16),
            dma((9,)),
            dma((1,)),
            dma((5,)),
            dma((5,)),
            pltpu.SemaphoreType.REGULAR((2,)),
        ],
        compiler_params=pltpu.CompilerParams(
            collective_id=0, has_side_effects=True, vmem_limit_bytes=57 * 1024 * 1024
        ),
    )(
        near_offsets.T,
        coupling_pattern.T,
        measured,
        cluster_perm,
        near_blocks,
        leaf_bases,
        local_transfer,
        local_coupling,
        root_transfer,
        top_blocks,
    )


def solution(mesh):
    return jax.shard_map(
        body,
        mesh=mesh,
        in_specs=(
            P(None, "leaf"),
            P("leaf", None),
            P("leaf", None),
            P("leaf", None, None),
            P("leaf", None),
            P("leaf", None, None),
            P("leaf", None),
            P("leaf", None, None),
            P("leaf", None),
            P(),
        ),
        out_specs=P(None, "leaf"),
        check_vma=False,
    )
```

```python
import jax
import jax.numpy as jnp
from jax import lax
from jax.experimental import pallas as pl
from jax.experimental.pallas import tpu as pltpu
from jax.sharding import PartitionSpec as P

F32 = jnp.float32
BF16 = jnp.bfloat16
MESH = pl.DeviceIdType.MESH
NRHS = 16
RANK = 64
LEAVES = 64
POINTS = 4096
SPAN = 256
CHUNKS = POINTS // SPAN
COARSE = POINTS // SPAN

UP_SLOT = {4: 0, 3: 16, 2: 24, 7: 28, 6: 32, 5: 34}
UP_COUNT = {4: 16, 3: 8, 2: 4, 7: 4, 6: 2, 5: 1}

NEAR_PEERS = (4, 5, 6, 7, 2, 3, 1)
Z_HOPS = (0, 1, 2, 3, 4, 3, 2, 3)
Y_HOPS = (0, 1, 2, 1)
FAR_PEERS = tuple(sorted(range(1, 32), key=lambda k: -Z_HOPS[k % 8] - Y_HOPS[k // 8]))


def nn(a, b):
    return lax.dot_general(a, b, (((1,), (0,)), ((), ())), preferred_element_type=F32)


def nt(a, b):
    return lax.dot_general(a, b, (((1,), (1,)), ((), ())), preferred_element_type=F32)


def flipped(index, mask):
    out = index
    for bit in range(8):
        if (mask >> bit) & 1:
            step = 1 << bit
            out = out + step * (1 - 2 * lax.rem(lax.div(index, step), 2))
    return out


def split(x):
    high = x.astype(BF16)
    return high, (x - high.astype(F32)).astype(BF16)


def stacked(x):
    return jnp.concatenate(split(x), axis=0)[:, :RANK]


def folded(x):
    return x[0:NRHS] + x[NRHS : 2 * NRHS]


def swapped(x):
    return pltpu.roll(x, RANK, axis=1)


def kernel(
    offsets_hbm,
    pattern_hbm,
    measured_hbm,
    perm_hbm,
    near_hbm,
    bases_hbm,
    transfer_hbm,
    coupling_hbm,
    root_hbm,
    top_hbm,
    out,
    offsets,
    pattern,
    measured,
    perm,
    near_blocks,
    bases,
    transfer,
    coupling,
    root_row,
    tops,
    climbs,
    group_up,
    local_map,
    up_map,
    reach,
    root_rows,
    root_wide,
    perm_rows,
    mix,
    mixed_order,
    mixed_points,
    basis,
    basis_pairs,
    onehot,
    points,
    coef,
    local_terms,
    near_part,
    fields,
    combined,
    edges,
    halo,
    first,
    first_coef,
    second,
    second_coef,
    in_sem,
    top_sem,
    send_sem,
    recv_sem,
    ready,
):
    me = lax.axis_index("leaf")
    right = lax.rem(me + 1, 256)
    left = lax.rem(me + 255, 256)
    low = lax.broadcasted_iota(jnp.int32, (NRHS, 128), 1) < RANK

    loads = [
        pltpu.make_async_copy(source, target, in_sem.at[i])
        for i, (source, target) in enumerate(
            [
                (perm_hbm, perm),
                (measured_hbm, measured),
                (bases_hbm, bases),
                (root_hbm, root_row),
                (transfer_hbm, transfer),
                (coupling_hbm, coupling),
                (near_hbm, near_blocks),
                (pattern_hbm, pattern),
                (offsets_hbm, offsets),
            ]
        )
    ]
    for load in loads[:4]:
        load.start()

    barrier = pltpu.get_barrier_semaphore()
    core = lax.rem(me, 2)
    place = lax.rem(me, 8)

    def tell(device):
        pl.semaphore_signal(barrier, inc=1, device_id=(device,), device_id_type=MESH)

    @pl.when(place == 7)
    def _():
        tell(right)

    @pl.when(place == 0)
    def _():
        tell(left)

    for k in (4, 2, 6):
        tell(flipped(me - core, k))

    @pl.when(core == 1)
    def _():
        tell(me - 1)

    for k in FAR_PEERS:
        tell(flipped(me - core + 1, 8 * k))

    loads[4].start()
    natural = lax.broadcasted_iota(jnp.int32, (SPAN, SPAN), 0)
    column = lax.broadcasted_iota(jnp.int32, (SPAN, SPAN), 1)
    within = lax.rem(column, RANK)
    wanted = column - within + 2 * lax.rem(within, 32) + lax.div(within, 32)
    mix[...] = jnp.where(natural == wanted, 1.0, 0.0).astype(BF16)
    loads[0].wait()
    for c in range(CHUNKS):
        perm_rows[c : c + 1, :] = perm[0:1, c * SPAN : (c + 1) * SPAN]
    order = perm_rows[...]
    digits = jnp.concatenate([lax.rem(order, SPAN), lax.div(order, SPAN)], axis=0)
    mixed = nn(digits.astype(F32).astype(BF16), mix[...])
    mixed_order[...] = mixed.astype(jnp.int32)
    fine_order = mixed.astype(BF16)
    numbers = natural.astype(F32).astype(BF16)
    one, zero = jnp.ones((SPAN, SPAN), BF16), jnp.zeros((SPAN, SPAN), BF16)

    loads[1].wait()
    loads[2].wait()
    loads[3].wait()
    group = lax.div(me, 8)
    top_loads = [
        pltpu.make_async_copy(top_hbm.at[pl.ds(start, count)], tops.at[pl.ds(at, count)], top_sem.at[0])
        for start, at, count in (
            (0, 0, 32),
            (32 + group, 32, 1),
            (64 + 2 * group, 33, 2),
            (128 + 4 * group, 35, 4),
        )
    ]
    for load in top_loads:
        load.start()
    for load in loads[5:]:
        load.start()
    for pair in range(32):
        root_rows[pair : pair + 1, :] = root_row[0:1, pair * 128 : (pair + 1) * 128].astype(F32)
    both = root_rows[...]
    turned = swapped(both)
    low_half = lax.broadcasted_iota(jnp.int32, (32, 128), 1) < RANK
    root_wide[pl.ds(0, 32, stride=2), :] = jnp.where(low_half, both, turned)
    root_wide[pl.ds(1, 32, stride=2), :] = jnp.where(low_half, turned, both)
    root_map = root_wide[...].astype(BF16)

    spread = jnp.concatenate(
        [measured[:, h * SPAN : (h + 1) * SPAN] for h in range(COARSE)], axis=0
    )
    for c in range(CHUNKS):
        at = slice(c * SPAN, (c + 1) * SPAN)
        hot = jnp.where(numbers == fine_order[c : c + 1, :], one, zero)
        onehot[:, at] = hot
        picked = nn(spread, hot)
        coarse = jnp.broadcast_to(mixed_order[COARSE + c : COARSE + c + 1, :], (NRHS, SPAN))
        chosen = picked[0:NRHS]
        for h in range(1, COARSE):
            chosen = jnp.where(coarse == h, picked[h * NRHS : (h + 1) * NRHS], chosen)
        mixed_points[:, at] = chosen.astype(BF16)

    loads[4].wait()
    low_rank = lax.broadcasted_iota(jnp.int32, (RANK, 128), 1) < RANK

    def opened(x):
        return x + swapped(x)

    def both_parts(x):
        high = x.astype(BF16).astype(F32)
        return jnp.where(low_rank, high, x - high).astype(BF16)

    def folded_rows(x):
        return x[0:RANK] + x[RANK : 2 * RANK]

    first_pair = transfer[0].astype(F32)
    maps = {
        2: jnp.where(low_rank, first_pair, 0.0).astype(BF16),
        3: jnp.where(low_rank, swapped(first_pair), 0.0).astype(BF16),
    }
    products = {}

    def multiply(slot):
        block = transfer[slot // 2 - 1]
        step = block[:, :RANK] if slot % 2 == 0 else block[:, RANK:]
        products[slot] = opened(nn(step, maps[slot // 2]))
        maps[slot] = both_parts(products[slot])
        if slot >= 16:
            local_map[slot - 16] = maps[slot]

    def through_root(slot):
        rows = jnp.concatenate(split(products[slot]), axis=0)[:, :RANK]
        up_map[slot - 8] = both_parts(folded_rows(nn(rows, root_map)))

    tasks = [(multiply, slot) for slot in range(4, 16)] + [(through_root, slot) for slot in range(8, 16)]

    turn = jnp.where(lax.rem(natural, 8) * 32 + lax.div(natural, 8) == column, 1.0, 0.0).astype(BF16)
    low_half = lax.broadcasted_iota(jnp.int32, (32, 128), 1) < RANK
    for side in range(2):
        rows = slice(side * 32, (side + 1) * 32)
        blocks = []
        for eight in range(4):
            taken = [bases[rows, (8 * eight + k) * 128 : (8 * eight + k + 1) * 128] for k in range(8)]
            blocks.append(nn(turn, jnp.concatenate(taken, axis=0)))
        for leaf in range(32):
            both = jnp.concatenate([block[leaf * 8 : (leaf + 1) * 8] for block in blocks], axis=0)
            turned = swapped(both)
            at = (side * 32 + leaf) * RANK
            basis[at : at + RANK, :] = jnp.concatenate(
                [jnp.where(low_half, both, turned), jnp.where(low_half, turned, both)], axis=0
            ).astype(BF16)
            if leaf % 3 == 0 and tasks:
                task, slot = tasks.pop(0)
                task(slot)

    quarter = lax.broadcasted_iota(jnp.int32, (NRHS, 256), 1) // RANK
    for four in range(LEAVES // 4):
        chunk = mixed_points[:, four * SPAN : (four + 1) * SPAN].astype(F32)
        block = jnp.concatenate(
            [jnp.where(quarter == k, chunk, 0.0) for k in range(4)], axis=0
        ).astype(BF16)
        result = nn(block, basis[four * 256 : (four + 1) * 256, :])
        for k in range(4):
            coef[64 + 4 * four + k] = jnp.concatenate(
                split(result[k * NRHS : (k + 1) * NRHS]), axis=0
            )

    def climb(parent):
        children = coef[pl.ds(2 * parent, 2)].reshape(64, 128)[:, :RANK]
        result = nn(children, transfer[parent - 1])
        mixed = jnp.where(low, folded(result[0:32]), folded(result[32:64]))
        return mixed + swapped(mixed)

    def climb_levels(levels):
        for level in levels:
            values = []
            for parent in range(1 << level, 2 << level):
                values.append(climb(parent))
                coef[parent] = jnp.concatenate(split(values[-1]), axis=0)
        return values

    def pairs_of(values):
        wide = [jnp.where(low, values[k], values[k + 1]) for k in range(0, len(values), 2)]
        return jnp.concatenate(split(jnp.concatenate(wide, axis=1)), axis=0)

    depth_3 = climb_levels((5, 4, 3))
    root_up = opened(folded(nn(pairs_of(depth_3), up_map[...].reshape(512, 128))))

    def packed(x):
        high = x.astype(BF16).astype(F32)
        return jnp.where(low, high, x - high).astype(BF16)

    def send(buffer, slot, mask, at):
        copy = pltpu.make_async_remote_copy(
            src_ref=buffer.at[0],
            dst_ref=buffer.at[slot],
            send_sem=send_sem.at[at],
            recv_sem=recv_sem.at[at],
            device_id=(flipped(me, mask),),
            device_id_type=MESH,
        )
        copy.start()

    def arrived(buffer, at):
        slots = buffer.at[pl.ds(1, buffer.shape[0] - 1)]
        pltpu.make_async_remote_copy(
            src_ref=slots,
            dst_ref=slots,
            send_sem=send_sem.at[at],
            recv_sem=recv_sem.at[at],
            device_id=(flipped(me, 1),),
            device_id_type=MESH,
        ).wait()

    first[0] = packed(root_up)

    def tell_other_core(at):
        pl.semaphore_signal(ready.at[at], inc=1, device_id=(flipped(me, 1),), device_id_type=MESH)

    @pl.when(core == 0)
    def _():
        pl.semaphore_wait(barrier, 7 + lax.div(7 - place, 7))
        tell_other_core(0)

    @pl.when(core == 1)
    def _():
        pl.semaphore_wait(ready.at[0], 1)

    for k in NEAR_PEERS:
        send(first, k, k, 0)
    @pl.when(core == 1)
    def _():
        pl.semaphore_wait(barrier, 62 + lax.div(place, 7))
        tell_other_core(1)

    for slot in range(16, 32):
        multiply(slot)
    climb_levels((2, 1))
    first_coef[0] = packed(climb(1))
    send(first_coef, 1, 1, 1)

    pltpu.make_async_copy(top_hbm.at[pl.ds(0, 39)], tops, top_sem.at[0]).wait()

    def top_row(level, k):
        if level == 0:
            return 1
        own = lax.div(me, 1 << (8 - level))
        if level < 5:
            return (1 << level) + flipped(own, k)
        if level == 5:
            return 32
        return (33 if level == 6 else 35) + flipped(lax.rem(own, 1 << (level - 5)), k)

    for level, count in UP_COUNT.items():
        for k in range(count):
            block = tops[top_row(level, k)].astype(F32)
            climbs[UP_SLOT[level] + k] = jnp.where(low_rank, swapped(block), block).astype(BF16)

    unmixed = nt(
        jnp.concatenate(
            [mixed_points[:, c * SPAN : (c + 1) * SPAN] for c in range(CHUNKS)], axis=0
        ),
        mix[...],
    )
    for m in range(LEAVES // 2):
        c, pair = m // 2, m % 2
        both = unmixed[c * NRHS : (c + 1) * NRHS, pair * 128 : (pair + 1) * 128]
        turned = swapped(both)
        points[2 * m + 2] = jnp.where(low, both, turned).astype(BF16)
        points[2 * m + 3] = jnp.where(low, turned, both).astype(BF16)
        if m == 0:
            edges[0] = both.astype(BF16)
        if m == LEAVES // 2 - 1:
            edges[1] = both.astype(BF16)

    halo_copies = [
        pltpu.make_async_remote_copy(
            src_ref=edges.at[side],
            dst_ref=halo.at[side],
            send_sem=send_sem.at[4],
            recv_sem=recv_sem.at[4],
            device_id=(target,),
            device_id_type=MESH,
        )
        for side, target in ((0, left), (1, right))
    ]
    for copy in halo_copies:
        copy.start()


    def couple(pair):
        sides = []
        for k in range(2):
            n = 2 * pair + k
            sides.append(
                jnp.concatenate(
                    [coef[pattern[0, n]][:, :RANK], coef[pattern[1, n]][:, RANK:]], axis=1
                )
            )
        blocks = coupling[pl.ds(2 * pair, 2)].reshape(128, 128)
        result = nt(jnp.concatenate(sides, axis=0), blocks)
        local_terms[pair + 1] = jnp.where(low, folded(result[0:32]), folded(result[32:64]))

    def near(pair):
        sides = []
        for k in range(2):
            leaf = 2 * pair + k
            at = [points[leaf + 2 + offsets[j, leaf]] for j in range(4)]
            sides.append(
                jnp.concatenate(
                    [at[0][:, :RANK], at[1][:, RANK:], at[2][:, :RANK], at[3][:, RANK:]], axis=1
                )
            )
        blocks = near_blocks[pl.ds(2 * pair, 2)].reshape(128, 256)
        result = nt(jnp.concatenate(sides, axis=0), blocks)
        near_part[pair] = jnp.where(low, result[0:NRHS], result[NRHS : 2 * NRHS])

    def lift(values, level):
        out = []
        for k in range(0, len(values), 2):
            both = jnp.where(low, values[k], values[k + 1])
            blocks = climbs[pl.ds(UP_SLOT[level] + k, 2)].reshape(128, 128)
            out.append(folded(nn(jnp.concatenate(split(both), axis=0), blocks)))
        return out

    def coupled(sibling, level):
        block = tops[top_row(level - 1, 0)]
        parts = stacked(sibling)
        to_left = folded(nt(parts, block[:, :RANK]))
        to_right = folded(nn(parts, block))[:, :RANK]
        odd = lax.rem(lax.div(me, 1 << (8 - level)), 2)
        return jnp.where(odd == 1, to_right, to_left)

    def received(buffer, k):
        return opened(buffer[k].astype(F32) + buffer[k + 1].astype(F32))

    for side in range(2):
        inner = split(nn(climbs[UP_SLOT[6] + side][:, :RANK], climbs[UP_SLOT[5]]))
        for k in (2 * side, 2 * side + 1):
            outer = climbs[UP_SLOT[7] + k][:, :RANK]
            high, rest = split(nn(outer, inner[0]) + nn(outer, inner[1]))
            group_up[k * RANK : (k + 1) * RANK, :] = jnp.where(
                low_rank, high.astype(F32), rest.astype(F32)
            ).astype(BF16)

    terms = {}
    arrived(first, 0)
    at_7 = [received(first, 2 * k) for k in range(4)]
    second[0] = packed(opened(folded(nn(pairs_of(at_7), group_up[...]))))

    @pl.when(core == 0)
    def _():
        pl.semaphore_wait(ready.at[1], 1)

    for k in FAR_PEERS:
        send(second, k, 8 * k, 2)
    at_6 = lift(at_7, 7)
    at_5 = lift(at_6, 6)[0]
    second_coef[0] = packed(at_5)
    send(second_coef, 1, 8, 3)
    def stacked_rows(x):
        return jnp.concatenate(split(x), axis=0)

    def times(x, block):
        return folded_rows(nn(stacked_rows(x), block))

    def times_turned(x, blocks):
        return folded_rows(nt(stacked_rows(x), blocks))

    def outward(x, level, k):
        blocks = climbs[pl.ds(UP_SLOT[level] + k, 2)].reshape(128, 128)[:, :RANK]
        return times_turned(x, blocks)

    def halves(x):
        return [x[:, :RANK], swapped(x)[:, :RANK]]

    down = {7: root_map[:, :RANK].astype(F32)}
    for level in range(6, 0, -1):
        down[level] = times(down[level + 1], climbs[UP_SLOT[level + 1]])[:, :RANK]

    def crossing(level):
        block = tops[top_row(level - 1, 0)]
        to_left = times(down[level], block)[:, :RANK]
        to_right = times_turned(down[level], block[:, :RANK])
        odd = lax.rem(lax.div(me, 1 << (8 - level)), 2)
        return jnp.where(odd == 1, to_right, to_left)

    by_pair = [jnp.concatenate([jnp.zeros((RANK, RANK), F32), crossing(4)], axis=1)]
    by_pair.append(outward(crossing(3), 4, 2))
    for j, part in enumerate(halves(outward(crossing(2), 3, 2))):
        by_pair.append(outward(part, 4, 4 + 2 * j))
    for i, outer in enumerate(halves(outward(crossing(1), 2, 2))):
        for j, part in enumerate(halves(outward(outer, 3, 4 + 2 * i))):
            by_pair.append(outward(part, 4, 8 + 4 * i + 2 * j))
    for p in range(8):
        reach[:, p * 128 : (p + 1) * 128] = stacked_rows(by_pair[p])

    arrived(first_coef, 1)
    terms[8] = coupled(opened(first_coef[1].astype(F32)), 8)
    terms[7] = coupled(at_7[1], 7)
    terms[6] = coupled(at_6[1], 6)

    for m in range(32):
        basis_pairs[m] = jnp.where(
            low_rank,
            basis[m * 128 : m * 128 + RANK, :].astype(F32),
            basis[m * 128 + RANK : (m + 1) * 128, :].astype(F32),
        ).astype(BF16)

    loads[5].wait()
    loads[7].wait()

    @pl.loop(0, 9)
    def _(step):
        for k in range(7):
            couple(7 * step + k)

    pltpu.make_async_remote_copy(
        src_ref=edges,
        dst_ref=halo,
        send_sem=send_sem.at[4],
        recv_sem=recv_sem.at[4],
        device_id=(left,),
        device_id_type=MESH,
    ).wait()
    for side, leaf, end in ((1, 0, 0), (0, 66, 255)):
        both = jnp.where(me == end, 0.0, halo[side].astype(F32))
        turned = swapped(both)
        points[leaf] = jnp.where(low, both, turned).astype(BF16)
        points[leaf + 1] = jnp.where(low, turned, both).astype(BF16)
    loads[6].wait()
    loads[8].wait()

    @pl.loop(0, 4)
    def _(step):
        for k in range(8):
            near(8 * step + k)

    arrived(second_coef, 3)
    def descend(parent, here, there):
        lhs = jnp.concatenate(
            [jnp.where(low, part, 0.0) for part in here]
            + [jnp.where(low, 0.0, part) for part in there],
            axis=0,
        ).astype(BF16)
        result = nt(lhs, transfer[parent - 1])
        fields[parent] = local_terms[parent] + side_by_side(result)

    def side_by_side(result):
        return jnp.concatenate([folded(result[0:32]), folded(result[32:64])], axis=1)

    def parts_of(x):
        high = x.astype(BF16).astype(F32)
        return high, x - high

    def descend_levels(levels):
        for level in levels:
            for q in range(1 << level, 2 << level):
                pair = fields[q]
                straight = parts_of(pair)
                crossed = parts_of(swapped(pair))
                descend(2 * q, straight, crossed)
                descend(2 * q + 1, crossed, straight)

    fields[1] = local_terms[1]
    descend_levels((0, 1, 2))

    naturals = jnp.concatenate([near_part[m] for m in range(LEAVES // 2)], axis=0)
    high, rest = split(naturals)
    mixer = mix[0:128, 0:128]
    turned = nn(high, mixer) + nn(rest, mixer)
    for m in range(LEAVES // 2):
        near_part[m] = turned[m * NRHS : (m + 1) * NRHS]

    field = coupled(opened(second_coef[1].astype(F32)), 5)
    for level in (6, 7):
        block = climbs[UP_SLOT[level]][:, :RANK]
        field = terms[level] + folded(nt(stacked(field), block))
    field = terms[8] + folded(nt(stacked(field), root_map[:, :RANK]))
    near_field = jnp.concatenate([field, field], axis=1)

    arrived(second, 2)
    at_4 = [received(second, 2 * k) for k in range(16)]
    root_field = near_field + opened(folded(nt(pairs_of(at_4), reach[...])))

    arriving = folded(
        nt(jnp.concatenate(split(root_field), axis=0), local_map[...].reshape(1024, 128))
    )
    for p in range(8, 16):
        fields[p] = fields[p] + arriving[:, (p - 8) * 128 : (p - 7) * 128]
    descend_levels((3, 4))

    for m in range(32):
        pair = fields[32 + m]
        high, rest = parts_of(pair)
        lhs = jnp.concatenate(
            [jnp.where(low, high, 0.0), jnp.where(low, rest, 0.0)]
            + [jnp.where(low, 0.0, high), jnp.where(low, 0.0, rest)],
            axis=0,
        ).astype(BF16)
        whole = near_part[m] + side_by_side(nt(lhs, basis_pairs[m]))
        combined[:, m * 128 : (m + 1) * 128] = jnp.concatenate(parts_of(whole), axis=0)

    total = jnp.zeros((COARSE * 32, SPAN), F32)
    for c in range(CHUNKS):
        at = slice(c * SPAN, (c + 1) * SPAN)
        coarse = jnp.broadcast_to(mixed_order[COARSE + c : COARSE + c + 1, :], (32, SPAN))
        values = combined[:, at]
        lhs = jnp.concatenate(
            [jnp.where(coarse == h, values, 0.0) for h in range(COARSE)], axis=0
        ).astype(BF16)
        total = total + nt(lhs, onehot[:, at])
    for h in range(COARSE):
        out[:, h * SPAN : (h + 1) * SPAN] = folded(total[h * 32 : (h + 1) * 32])


def body(
    measured,
    cluster_perm,
    near_offsets,
    near_blocks,
    leaf_bases,
    local_transfer,
    coupling_pattern,
    local_coupling,
    root_transfer,
    top_blocks,
):
    hbm = pl.BlockSpec(memory_space=pl.ANY)
    dma = pltpu.SemaphoreType.DMA
    return pl.pallas_call(
        kernel,
        out_shape=pltpu.VMEM((NRHS, POINTS), F32),
        in_specs=[hbm] * 10,
        out_specs=pl.BlockSpec(memory_space=pltpu.VMEM),
        scratch_shapes=[
            pltpu.SMEM((4, 64), jnp.int32),
            pltpu.SMEM((2, 126), jnp.int32),
            pltpu.VMEM((NRHS, POINTS), BF16),
            pltpu.VMEM((1, POINTS), jnp.int32),
            pltpu.VMEM((64, 64, 256), BF16),
            pltpu.VMEM((64, 4096), BF16),
            pltpu.VMEM((63, 64, 128), BF16),
            pltpu.VMEM((126, 64, 128), BF16),
            pltpu.VMEM((1, 4096), BF16),
            pltpu.VMEM((39, 64, 128), BF16),
            pltpu.VMEM((35, 64, 128), BF16),
            pltpu.VMEM((256, 128), BF16),
            pltpu.VMEM((16, 64, 128), BF16),
            pltpu.VMEM((8, 64, 128), BF16),
            pltpu.VMEM((128, 1024), BF16),
            pltpu.VMEM((32, 128), F32),
            pltpu.VMEM((64, 128), F32),
            pltpu.VMEM((CHUNKS, SPAN), jnp.int32),
            pltpu.VMEM((SPAN, SPAN), BF16),
            pltpu.VMEM((2 * CHUNKS, SPAN), jnp.int32),
            pltpu.VMEM((NRHS, POINTS), BF16),
            pltpu.VMEM((4096, 128), BF16),
            pltpu.VMEM((32, 64, 128), BF16),
            pltpu.VMEM((SPAN, POINTS), BF16),
            pltpu.VMEM((68, NRHS, 128), BF16),
            pltpu.VMEM((128, 2 * NRHS, 128), BF16),
            pltpu.VMEM((64, NRHS, 128), F32),
            pltpu.VMEM((32, NRHS, 128), F32),
            pltpu.VMEM((64, NRHS, 128), F32),
            pltpu.VMEM((2 * NRHS, POINTS), F32),
            pltpu.VMEM((2, NRHS, 128), BF16),
            pltpu.VMEM((2, NRHS, 128), BF16),
            pltpu.VMEM((8, NRHS, 128), BF16),
            pltpu.VMEM((2, NRHS, 128), BF16),
            pltpu.VMEM((32, NRHS, 128), BF16),
            pltpu.VMEM((2, NRHS, 128), BF16),
            dma((9,)),
            dma((1,)),
            dma((5,)),
            dma((5,)),
            pltpu.SemaphoreType.REGULAR((2,)),
        ],
        compiler_params=pltpu.CompilerParams(
            collective_id=0, has_side_effects=True, vmem_limit_bytes=57 * 1024 * 1024
        ),
    )(
        near_offsets.T,
        coupling_pattern.T,
        measured,
        cluster_perm,
        near_blocks,
        leaf_bases,
        local_transfer,
        local_coupling,
        root_transfer,
        top_blocks,
    )


def solution(mesh):
    return jax.shard_map(
        body,
        mesh=mesh,
        in_specs=(
            P(None, "leaf"),
            P("leaf", None),
            P("leaf", None),
            P("leaf", None, None),
            P("leaf", None),
            P("leaf", None, None),
            P("leaf", None),
            P("leaf", None, None),
            P("leaf", None),
            P(),
        ),
        out_specs=P(None, "leaf"),
        check_vma=False,
    )
```

```python
import jax
import jax.numpy as jnp
from jax import lax
from jax.experimental import pallas as pl
from jax.experimental.pallas import tpu as pltpu
from jax.sharding import PartitionSpec as P

F32 = jnp.float32
BF16 = jnp.bfloat16
MESH = pl.DeviceIdType.MESH
NRHS = 16
RANK = 64
LEAVES = 64
POINTS = 4096
SPAN = 256
CHUNKS = POINTS // SPAN
COARSE = POINTS // SPAN

UP_SLOT = {4: 0, 3: 16, 2: 24, 7: 28, 6: 32, 5: 34}
UP_COUNT = {4: 16, 3: 8, 2: 4, 7: 4, 6: 2, 5: 1}

NEAR_PEERS = (4, 5, 6, 7, 2, 3, 1)
Z_HOPS = (0, 1, 2, 3, 4, 3, 2, 3)
Y_HOPS = (0, 1, 2, 1)
FAR_PEERS = tuple(sorted(range(1, 32), key=lambda k: -Z_HOPS[k % 8] - Y_HOPS[k // 8]))


def nn(a, b):
    return lax.dot_general(a, b, (((1,), (0,)), ((), ())), preferred_element_type=F32)


def nt(a, b):
    return lax.dot_general(a, b, (((1,), (1,)), ((), ())), preferred_element_type=F32)


def flipped(index, mask):
    out = index
    for bit in range(8):
        if (mask >> bit) & 1:
            step = 1 << bit
            out = out + step * (1 - 2 * lax.rem(lax.div(index, step), 2))
    return out


def split(x):
    high = x.astype(BF16)
    return high, (x - high.astype(F32)).astype(BF16)


def stacked(x):
    return jnp.concatenate(split(x), axis=0)[:, :RANK]


def folded(x):
    return x[0:NRHS] + x[NRHS : 2 * NRHS]


def swapped(x):
    return pltpu.roll(x, RANK, axis=1)


def kernel(
    offsets_hbm,
    pattern_hbm,
    measured_hbm,
    perm_hbm,
    near_hbm,
    bases_hbm,
    transfer_hbm,
    coupling_hbm,
    root_hbm,
    top_hbm,
    out,
    offsets,
    pattern,
    measured,
    perm,
    near_blocks,
    bases,
    transfer,
    coupling,
    root_row,
    tops,
    climbs,
    group_up,
    local_map,
    up_map,
    reach,
    root_rows,
    root_wide,
    perm_rows,
    mix,
    mixed_order,
    mixed_points,
    basis,
    basis_pairs,
    onehot,
    points,
    coef,
    local_terms,
    near_part,
    fields,
    combined,
    edges,
    halo,
    first,
    first_coef,
    second,
    second_coef,
    in_sem,
    top_sem,
    send_sem,
    recv_sem,
    ready,
):
    me = lax.axis_index("leaf")
    right = lax.rem(me + 1, 256)
    left = lax.rem(me + 255, 256)
    low = lax.broadcasted_iota(jnp.int32, (NRHS, 128), 1) < RANK

    loads = [
        pltpu.make_async_copy(source, target, in_sem.at[i])
        for i, (source, target) in enumerate(
            [
                (perm_hbm, perm),
                (measured_hbm, measured),
                (bases_hbm, bases),
                (root_hbm, root_row),
                (transfer_hbm, transfer),
                (coupling_hbm, coupling),
                (near_hbm, near_blocks),
                (pattern_hbm, pattern),
                (offsets_hbm, offsets),
            ]
        )
    ]
    for load in loads[:4]:
        load.start()

    barrier = pltpu.get_barrier_semaphore()
    core = lax.rem(me, 2)
    place = lax.rem(me, 8)

    def tell(device):
        pl.semaphore_signal(barrier, inc=1, device_id=(device,), device_id_type=MESH)

    @pl.when(place == 7)
    def _():
        tell(right)

    @pl.when(place == 0)
    def _():
        tell(left)

    for k in (4, 2, 6):
        tell(flipped(me - core, k))

    @pl.when(core == 1)
    def _():
        tell(me - 1)

    for k in FAR_PEERS:
        tell(flipped(me - core + 1, 8 * k))

    loads[4].start()
    natural = lax.broadcasted_iota(jnp.int32, (SPAN, SPAN), 0)
    column = lax.broadcasted_iota(jnp.int32, (SPAN, SPAN), 1)
    within = lax.rem(column, RANK)
    wanted = column - within + 2 * lax.rem(within, 32) + lax.div(within, 32)
    mix[...] = jnp.where(natural == wanted, 1.0, 0.0).astype(BF16)
    loads[0].wait()
    for c in range(CHUNKS):
        perm_rows[c : c + 1, :] = perm[0:1, c * SPAN : (c + 1) * SPAN]
    order = perm_rows[...]
    digits = jnp.concatenate([lax.rem(order, SPAN), lax.div(order, SPAN)], axis=0)
    mixed = nn(digits.astype(F32).astype(BF16), mix[...])
    mixed_order[...] = mixed.astype(jnp.int32)
    fine_order = mixed.astype(BF16)
    numbers = natural.astype(F32).astype(BF16)
    one, zero = jnp.ones((SPAN, SPAN), BF16), jnp.zeros((SPAN, SPAN), BF16)

    loads[1].wait()
    loads[2].wait()
    loads[3].wait()
    group = lax.div(me, 8)
    top_loads = [
        pltpu.make_async_copy(top_hbm.at[pl.ds(start, count)], tops.at[pl.ds(at, count)], top_sem.at[0])
        for start, at, count in (
            (0, 0, 32),
            (32 + group, 32, 1),
            (64 + 2 * group, 33, 2),
            (128 + 4 * group, 35, 4),
        )
    ]
    for load in top_loads:
        load.start()
    for load in loads[5:]:
        load.start()
    for pair in range(32):
        root_rows[pair : pair + 1, :] = root_row[0:1, pair * 128 : (pair + 1) * 128].astype(F32)
    both = root_rows[...]
    turned = swapped(both)
    low_half = lax.broadcasted_iota(jnp.int32, (32, 128), 1) < RANK
    root_wide[pl.ds(0, 32, stride=2), :] = jnp.where(low_half, both, turned)
    root_wide[pl.ds(1, 32, stride=2), :] = jnp.where(low_half, turned, both)
    root_map = root_wide[...].astype(BF16)

    spread = jnp.concatenate(
        [measured[:, h * SPAN : (h + 1) * SPAN] for h in range(COARSE)], axis=0
    )
    for c in range(CHUNKS):
        at = slice(c * SPAN, (c + 1) * SPAN)
        hot = jnp.where(numbers == fine_order[c : c + 1, :], one, zero)
        onehot[:, at] = hot
        picked = nn(spread, hot)
        coarse = jnp.broadcast_to(mixed_order[COARSE + c : COARSE + c + 1, :], (NRHS, SPAN))
        chosen = picked[0:NRHS]
        for h in range(1, COARSE):
            chosen = jnp.where(coarse == h, picked[h * NRHS : (h + 1) * NRHS], chosen)
        mixed_points[:, at] = chosen.astype(BF16)

    loads[4].wait()
    low_rank = lax.broadcasted_iota(jnp.int32, (RANK, 128), 1) < RANK

    def opened(x):
        return x + swapped(x)

    def both_parts(x):
        high = x.astype(BF16).astype(F32)
        return jnp.where(low_rank, high, x - high).astype(BF16)

    def folded_rows(x):
        return x[0:RANK] + x[RANK : 2 * RANK]

    first_pair = transfer[0].astype(F32)
    maps = {
        2: jnp.where(low_rank, first_pair, 0.0).astype(BF16),
        3: jnp.where(low_rank, swapped(first_pair), 0.0).astype(BF16),
    }
    products = {}

    def multiply(slot):
        block = transfer[slot // 2 - 1]
        step = block[:, :RANK] if slot % 2 == 0 else block[:, RANK:]
        products[slot] = opened(nn(step, maps[slot // 2]))
        maps[slot] = both_parts(products[slot])
        if slot >= 16:
            local_map[slot - 16] = maps[slot]

    def through_root(slot):
        rows = jnp.concatenate(split(products[slot]), axis=0)[:, :RANK]
        up_map[slot - 8] = both_parts(folded_rows(nn(rows, root_map)))

    tasks = [(multiply, slot) for slot in range(4, 16)] + [(through_root, slot) for slot in range(8, 16)]

    turn = jnp.where(lax.rem(natural, 8) * 32 + lax.div(natural, 8) == column, 1.0, 0.0).astype(BF16)
    low_half = lax.broadcasted_iota(jnp.int32, (32, 128), 1) < RANK
    for side in range(2):
        rows = slice(side * 32, (side + 1) * 32)
        blocks = []
        for eight in range(4):
            taken = [bases[rows, (8 * eight + k) * 128 : (8 * eight + k + 1) * 128] for k in range(8)]
            blocks.append(nn(turn, jnp.concatenate(taken, axis=0)))
        for leaf in range(32):
            both = jnp.concatenate([block[leaf * 8 : (leaf + 1) * 8] for block in blocks], axis=0)
            turned = swapped(both)
            at = (side * 32 + leaf) * RANK
            basis[at : at + RANK, :] = jnp.concatenate(
                [jnp.where(low_half, both, turned), jnp.where(low_half, turned, both)], axis=0
            ).astype(BF16)
            if leaf % 3 == 0 and tasks:
                task, slot = tasks.pop(0)
                task(slot)

    quarter = lax.broadcasted_iota(jnp.int32, (NRHS, 256), 1) // RANK
    for four in range(LEAVES // 4):
        chunk = mixed_points[:, four * SPAN : (four + 1) * SPAN].astype(F32)
        block = jnp.concatenate(
            [jnp.where(quarter == k, chunk, 0.0) for k in range(4)], axis=0
        ).astype(BF16)
        result = nn(block, basis[four * 256 : (four + 1) * 256, :])
        for k in range(4):
            coef[64 + 4 * four + k] = jnp.concatenate(
                split(result[k * NRHS : (k + 1) * NRHS]), axis=0
            )

    def climb(parent):
        children = coef[pl.ds(2 * parent, 2)].reshape(64, 128)[:, :RANK]
        result = nn(children, transfer[parent - 1])
        mixed = jnp.where(low, folded(result[0:32]), folded(result[32:64]))
        return mixed + swapped(mixed)

    def climb_levels(levels):
        for level in levels:
            values = []
            for parent in range(1 << level, 2 << level):
                values.append(climb(parent))
                coef[parent] = jnp.concatenate(split(values[-1]), axis=0)
        return values

    def pairs_of(values):
        wide = [jnp.where(low, values[k], values[k + 1]) for k in range(0, len(values), 2)]
        return jnp.concatenate(split(jnp.concatenate(wide, axis=1)), axis=0)

    depth_3 = climb_levels((5, 4, 3))
    root_up = opened(folded(nn(pairs_of(depth_3), up_map[...].reshape(512, 128))))

    def packed(x):
        high = x.astype(BF16).astype(F32)
        return jnp.where(low, high, x - high).astype(BF16)

    def send(buffer, slot, mask, at):
        copy = pltpu.make_async_remote_copy(
            src_ref=buffer.at[0],
            dst_ref=buffer.at[slot],
            send_sem=send_sem.at[at],
            recv_sem=recv_sem.at[at],
            device_id=(flipped(me, mask),),
            device_id_type=MESH,
        )
        copy.start()

    def arrived(buffer, at):
        slots = buffer.at[pl.ds(1, buffer.shape[0] - 1)]
        pltpu.make_async_remote_copy(
            src_ref=slots,
            dst_ref=slots,
            send_sem=send_sem.at[at],
            recv_sem=recv_sem.at[at],
            device_id=(flipped(me, 1),),
            device_id_type=MESH,
        ).wait()

    first[0] = packed(root_up)

    def tell_other_core(at):
        pl.semaphore_signal(ready.at[at], inc=1, device_id=(flipped(me, 1),), device_id_type=MESH)

    @pl.when(core == 0)
    def _():
        pl.semaphore_wait(barrier, 7 + lax.div(7 - place, 7))
        tell_other_core(0)

    @pl.when(core == 1)
    def _():
        pl.semaphore_wait(ready.at[0], 1)

    for k in NEAR_PEERS:
        send(first, k, k, 0)
    @pl.when(core == 1)
    def _():
        pl.semaphore_wait(barrier, 62 + lax.div(place, 7))
        tell_other_core(1)

    for slot in range(16, 32):
        multiply(slot)
    climb_levels((2, 1))
    first_coef[0] = packed(climb(1))
    send(first_coef, 1, 1, 1)

    pltpu.make_async_copy(top_hbm.at[pl.ds(0, 39)], tops, top_sem.at[0]).wait()

    def top_row(level, k):
        if level == 0:
            return 1
        own = lax.div(me, 1 << (8 - level))
        if level < 5:
            return (1 << level) + flipped(own, k)
        if level == 5:
            return 32
        return (33 if level == 6 else 35) + flipped(lax.rem(own, 1 << (level - 5)), k)

    for level, count in UP_COUNT.items():
        for k in range(count):
            block = tops[top_row(level, k)].astype(F32)
            climbs[UP_SLOT[level] + k] = jnp.where(low_rank, swapped(block), block).astype(BF16)

    unmixed = nt(
        jnp.concatenate(
            [mixed_points[:, c * SPAN : (c + 1) * SPAN] for c in range(CHUNKS)], axis=0
        ),
        mix[...],
    )
    for m in range(LEAVES // 2):
        c, pair = m // 2, m % 2
        both = unmixed[c * NRHS : (c + 1) * NRHS, pair * 128 : (pair + 1) * 128]
        turned = swapped(both)
        points[2 * m + 2] = jnp.where(low, both, turned).astype(BF16)
        points[2 * m + 3] = jnp.where(low, turned, both).astype(BF16)
        if m == 0:
            edges[0] = both.astype(BF16)
        if m == LEAVES // 2 - 1:
            edges[1] = both.astype(BF16)

    halo_copies = [
        pltpu.make_async_remote_copy(
            src_ref=edges.at[side],
            dst_ref=halo.at[side],
            send_sem=send_sem.at[4],
            recv_sem=recv_sem.at[4],
            device_id=(target,),
            device_id_type=MESH,
        )
        for side, target in ((0, left), (1, right))
    ]
    for copy in halo_copies:
        copy.start()


    def couple(pair):
        sides = []
        for k in range(2):
            n = 2 * pair + k
            sides.append(
                jnp.concatenate(
                    [coef[pattern[0, n]][:, :RANK], coef[pattern[1, n]][:, RANK:]], axis=1
                )
            )
        blocks = coupling[pl.ds(2 * pair, 2)].reshape(128, 128)
        result = nt(jnp.concatenate(sides, axis=0), blocks)
        local_terms[pair + 1] = jnp.where(low, folded(result[0:32]), folded(result[32:64]))

    def near(pair):
        sides = []
        for k in range(2):
            leaf = 2 * pair + k
            at = [points[leaf + 2 + offsets[j, leaf]] for j in range(4)]
            sides.append(
                jnp.concatenate(
                    [at[0][:, :RANK], at[1][:, RANK:], at[2][:, :RANK], at[3][:, RANK:]], axis=1
                )
            )
        blocks = near_blocks[pl.ds(2 * pair, 2)].reshape(128, 256)
        result = nt(jnp.concatenate(sides, axis=0), blocks)
        near_part[pair] = jnp.where(low, result[0:NRHS], result[NRHS : 2 * NRHS])

    def lift(values, level):
        out = []
        for k in range(0, len(values), 2):
            both = jnp.where(low, values[k], values[k + 1])
            blocks = climbs[pl.ds(UP_SLOT[level] + k, 2)].reshape(128, 128)
            out.append(folded(nn(jnp.concatenate(split(both), axis=0), blocks)))
        return out

    def coupled(sibling, level):
        block = tops[top_row(level - 1, 0)]
        parts = stacked(sibling)
        to_left = folded(nt(parts, block[:, :RANK]))
        to_right = folded(nn(parts, block))[:, :RANK]
        odd = lax.rem(lax.div(me, 1 << (8 - level)), 2)
        return jnp.where(odd == 1, to_right, to_left)

    def received(buffer, k):
        return opened(buffer[k].astype(F32) + buffer[k + 1].astype(F32))

    for side in range(2):
        inner = split(nn(climbs[UP_SLOT[6] + side][:, :RANK], climbs[UP_SLOT[5]]))
        for k in (2 * side, 2 * side + 1):
            outer = climbs[UP_SLOT[7] + k][:, :RANK]
            high, rest = split(nn(outer, inner[0]) + nn(outer, inner[1]))
            group_up[k * RANK : (k + 1) * RANK, :] = jnp.where(
                low_rank, high.astype(F32), rest.astype(F32)
            ).astype(BF16)

    terms = {}
    arrived(first, 0)
    at_7 = [received(first, 2 * k) for k in range(4)]
    second[0] = packed(opened(folded(nn(pairs_of(at_7), group_up[...]))))

    @pl.when(core == 0)
    def _():
        pl.semaphore_wait(ready.at[1], 1)

    for k in FAR_PEERS:
        send(second, k, 8 * k, 2)
    at_6 = lift(at_7, 7)
    at_5 = lift(at_6, 6)[0]
    second_coef[0] = packed(at_5)
    send(second_coef, 1, 8, 3)
    def stacked_rows(x):
        return jnp.concatenate(split(x), axis=0)

    def times(x, block):
        return folded_rows(nn(stacked_rows(x), block))

    def times_turned(x, blocks):
        return folded_rows(nt(stacked_rows(x), blocks))

    def outward(x, level, k):
        blocks = climbs[pl.ds(UP_SLOT[level] + k, 2)].reshape(128, 128)[:, :RANK]
        return times_turned(x, blocks)

    def halves(x):
        return [x[:, :RANK], swapped(x)[:, :RANK]]

    down = {7: root_map[:, :RANK].astype(F32)}
    for level in range(6, 0, -1):
        down[level] = times(down[level + 1], climbs[UP_SLOT[level + 1]])[:, :RANK]

    def crossing(level):
        block = tops[top_row(level - 1, 0)]
        to_left = times(down[level], block)[:, :RANK]
        to_right = times_turned(down[level], block[:, :RANK])
        odd = lax.rem(lax.div(me, 1 << (8 - level)), 2)
        return jnp.where(odd == 1, to_right, to_left)

    by_pair = [jnp.concatenate([jnp.zeros((RANK, RANK), F32), crossing(4)], axis=1)]
    by_pair.append(outward(crossing(3), 4, 2))
    for j, part in enumerate(halves(outward(crossing(2), 3, 2))):
        by_pair.append(outward(part, 4, 4 + 2 * j))
    for i, outer in enumerate(halves(outward(crossing(1), 2, 2))):
        for j, part in enumerate(halves(outward(outer, 3, 4 + 2 * i))):
            by_pair.append(outward(part, 4, 8 + 4 * i + 2 * j))
    for p in range(8):
        reach[:, p * 128 : (p + 1) * 128] = stacked_rows(by_pair[p])

    arrived(first_coef, 1)
    terms[8] = coupled(opened(first_coef[1].astype(F32)), 8)
    terms[7] = coupled(at_7[1], 7)
    terms[6] = coupled(at_6[1], 6)

    for m in range(32):
        basis_pairs[m] = jnp.where(
            low_rank,
            basis[m * 128 : m * 128 + RANK, :].astype(F32),
            basis[m * 128 + RANK : (m + 1) * 128, :].astype(F32),
        ).astype(BF16)

    loads[5].wait()
    loads[7].wait()

    @pl.loop(0, 3)
    def _(step):
        for k in range(21):
            couple(21 * step + k)

    pltpu.make_async_remote_copy(
        src_ref=edges,
        dst_ref=halo,
        send_sem=send_sem.at[4],
        recv_sem=recv_sem.at[4],
        device_id=(left,),
        device_id_type=MESH,
    ).wait()
    for side, leaf, end in ((1, 0, 0), (0, 66, 255)):
        both = jnp.where(me == end, 0.0, halo[side].astype(F32))
        turned = swapped(both)
        points[leaf] = jnp.where(low, both, turned).astype(BF16)
        points[leaf + 1] = jnp.where(low, turned, both).astype(BF16)
    loads[6].wait()
    loads[8].wait()

    @pl.loop(0, 2)
    def _(step):
        for k in range(16):
            near(16 * step + k)

    arrived(second_coef, 3)
    def descend(parent, here, there):
        lhs = jnp.concatenate(
            [jnp.where(low, part, 0.0) for part in here]
            + [jnp.where(low, 0.0, part) for part in there],
            axis=0,
        ).astype(BF16)
        result = nt(lhs, transfer[parent - 1])
        fields[parent] = local_terms[parent] + side_by_side(result)

    def side_by_side(result):
        return jnp.concatenate([folded(result[0:32]), folded(result[32:64])], axis=1)

    def parts_of(x):
        high = x.astype(BF16).astype(F32)
        return high, x - high

    def descend_levels(levels):
        for level in levels:
            for q in range(1 << level, 2 << level):
                pair = fields[q]
                straight = parts_of(pair)
                crossed = parts_of(swapped(pair))
                descend(2 * q, straight, crossed)
                descend(2 * q + 1, crossed, straight)

    fields[1] = local_terms[1]
    descend_levels((0, 1, 2))

    naturals = jnp.concatenate([near_part[m] for m in range(LEAVES // 2)], axis=0)
    high, rest = split(naturals)
    mixer = mix[0:128, 0:128]
    turned = nn(high, mixer) + nn(rest, mixer)
    for m in range(LEAVES // 2):
        near_part[m] = turned[m * NRHS : (m + 1) * NRHS]

    field = coupled(opened(second_coef[1].astype(F32)), 5)
    for level in (6, 7):
        block = climbs[UP_SLOT[level]][:, :RANK]
        field = terms[level] + folded(nt(stacked(field), block))
    field = terms[8] + folded(nt(stacked(field), root_map[:, :RANK]))
    near_field = jnp.concatenate([field, field], axis=1)

    arrived(second, 2)
    at_4 = [received(second, 2 * k) for k in range(16)]
    root_field = near_field + opened(folded(nt(pairs_of(at_4), reach[...])))

    arriving = folded(
        nt(jnp.concatenate(split(root_field), axis=0), local_map[...].reshape(1024, 128))
    )
    for p in range(8, 16):
        fields[p] = fields[p] + arriving[:, (p - 8) * 128 : (p - 7) * 128]
    descend_levels((3, 4))

    for m in range(32):
        pair = fields[32 + m]
        high, rest = parts_of(pair)
        lhs = jnp.concatenate(
            [jnp.where(low, high, 0.0), jnp.where(low, rest, 0.0)]
            + [jnp.where(low, 0.0, high), jnp.where(low, 0.0, rest)],
            axis=0,
        ).astype(BF16)
        whole = near_part[m] + side_by_side(nt(lhs, basis_pairs[m]))
        combined[:, m * 128 : (m + 1) * 128] = jnp.concatenate(parts_of(whole), axis=0)

    total = jnp.zeros((COARSE * 32, SPAN), F32)
    for c in range(CHUNKS):
        at = slice(c * SPAN, (c + 1) * SPAN)
        coarse = jnp.broadcast_to(mixed_order[COARSE + c : COARSE + c + 1, :], (32, SPAN))
        values = combined[:, at]
        lhs = jnp.concatenate(
            [jnp.where(coarse == h, values, 0.0) for h in range(COARSE)], axis=0
        ).astype(BF16)
        total = total + nt(lhs, onehot[:, at])
    for h in range(COARSE):
        out[:, h * SPAN : (h + 1) * SPAN] = folded(total[h * 32 : (h + 1) * 32])


def body(
    measured,
    cluster_perm,
    near_offsets,
    near_blocks,
    leaf_bases,
    local_transfer,
    coupling_pattern,
    local_coupling,
    root_transfer,
    top_blocks,
):
    hbm = pl.BlockSpec(memory_space=pl.ANY)
    dma = pltpu.SemaphoreType.DMA
    return pl.pallas_call(
        kernel,
        out_shape=pltpu.VMEM((NRHS, POINTS), F32),
        in_specs=[hbm] * 10,
        out_specs=pl.BlockSpec(memory_space=pltpu.VMEM),
        scratch_shapes=[
            pltpu.SMEM((4, 64), jnp.int32),
            pltpu.SMEM((2, 126), jnp.int32),
            pltpu.VMEM((NRHS, POINTS), BF16),
            pltpu.VMEM((1, POINTS), jnp.int32),
            pltpu.VMEM((64, 64, 256), BF16),
            pltpu.VMEM((64, 4096), BF16),
            pltpu.VMEM((63, 64, 128), BF16),
            pltpu.VMEM((126, 64, 128), BF16),
            pltpu.VMEM((1, 4096), BF16),
            pltpu.VMEM((39, 64, 128), BF16),
            pltpu.VMEM((35, 64, 128), BF16),
            pltpu.VMEM((256, 128), BF16),
            pltpu.VMEM((16, 64, 128), BF16),
            pltpu.VMEM((8, 64, 128), BF16),
            pltpu.VMEM((128, 1024), BF16),
            pltpu.VMEM((32, 128), F32),
            pltpu.VMEM((64, 128), F32),
            pltpu.VMEM((CHUNKS, SPAN), jnp.int32),
            pltpu.VMEM((SPAN, SPAN), BF16),
            pltpu.VMEM((2 * CHUNKS, SPAN), jnp.int32),
            pltpu.VMEM((NRHS, POINTS), BF16),
            pltpu.VMEM((4096, 128), BF16),
            pltpu.VMEM((32, 64, 128), BF16),
            pltpu.VMEM((SPAN, POINTS), BF16),
            pltpu.VMEM((68, NRHS, 128), BF16),
            pltpu.VMEM((128, 2 * NRHS, 128), BF16),
            pltpu.VMEM((64, NRHS, 128), F32),
            pltpu.VMEM((32, NRHS, 128), F32),
            pltpu.VMEM((64, NRHS, 128), F32),
            pltpu.VMEM((2 * NRHS, POINTS), F32),
            pltpu.VMEM((2, NRHS, 128), BF16),
            pltpu.VMEM((2, NRHS, 128), BF16),
            pltpu.VMEM((8, NRHS, 128), BF16),
            pltpu.VMEM((2, NRHS, 128), BF16),
            pltpu.VMEM((32, NRHS, 128), BF16),
            pltpu.VMEM((2, NRHS, 128), BF16),
            dma((9,)),
            dma((1,)),
            dma((5,)),
            dma((5,)),
            pltpu.SemaphoreType.REGULAR((2,)),
        ],
        compiler_params=pltpu.CompilerParams(
            collective_id=0, has_side_effects=True, vmem_limit_bytes=57 * 1024 * 1024
        ),
    )(
        near_offsets.T,
        coupling_pattern.T,
        measured,
        cluster_perm,
        near_blocks,
        leaf_bases,
        local_transfer,
        local_coupling,
        root_transfer,
        top_blocks,
    )


def solution(mesh):
    return jax.shard_map(
        body,
        mesh=mesh,
        in_specs=(
            P(None, "leaf"),
            P("leaf", None),
            P("leaf", None),
            P("leaf", None, None),
            P("leaf", None),
            P("leaf", None, None),
            P("leaf", None),
            P("leaf", None, None),
            P("leaf", None),
            P(),
        ),
        out_specs=P(None, "leaf"),
        check_vma=False,
    )
```
